256 devices in a mesh: tm: 32 (over y_hi, z, core), region: 8 (over y_lo, x).
Axes of the slice: x: 4, y: 4 (y_hi: 2, y_lo: 2; y = y_hi * 2 + y_lo), z: 8, core: 2. Of those that a mesh axis runs over, the one named last changes fastest.
Arguments:
- flux_init: float32 [128, 256, 128], P('region', 'tm'), may hold values from -6 to 6
- penalty: float32 [128, 256, 128], P('region', 'tm'), may hold values from 0.05 to 0.5
- observed: float32 [262144], P(('tm', 'region')), may hold values from -12 to 12
- footprint: bfloat16 [10240, 128, 1024], P(('tm', 'region')), may hold values from -0.1875 to 0.1875
- tile_index: int32 [10240, 4], P(('tm', 'region')), may hold values from 0 to 127, as said below
Outputs:
- flux: float32 [128, 256, 128], P('region', 'tm')
The draws below stay inside these ranges and needn't reach their ends.
Inputs may be any that keep to these rules, and one draw needn't show every extreme that they name: `tile_index`: each tile slot's entries are its observation block (below 8), how many windows back in time its flux block lies (below 4), its grid row (below 128) and a live flag of 0 or 1. On each device the live slots come first, at least half of its 40 slots are live, and some device has all 40 live.
All inputs are finite; a program needn't handle non-finite values.
Results may differ from the reference program's by a relative error of at most 0.0053.
Values may be sent and summed in bfloat16 or wider, within the bound.
A program may use at most 64 MiB of HBM per device.

```python
import math
import jax
import jax.numpy as jnp
from jax import lax

GY = 128
OB = 128
NOB = 8
NTILE = 40
LAG = 4
ITERS = 2
HOURS = 256
GX = 128
K = 1024
TILES = 10240
OBS = 262144
N_TM = 32
N_REGION = 8


def draw_tile_index(key, part):
    devices_all = TILES // NTILE
    first, second, third, fourth, fifth = jax.random.split(jax.random.fold_in(key, 17), 5)
    row_block = jax.random.randint(first, (devices_all, NTILE), 0, NOB)
    offset = jax.random.randint(second, (devices_all, NTILE), 0, LAG)
    grid_row = jax.random.randint(third, (devices_all, NTILE), 0, GX)
    counts = jax.random.randint(fourth, (devices_all,), (NTILE + 1) // 2, NTILE + 1)
    fullest = jax.random.randint(fifth, (), 0, devices_all)
    counts = jnp.where(jnp.arange(devices_all) == fullest, NTILE, counts)
    live_flag = (jnp.arange(NTILE)[None, :] < counts[:, None]).astype(jnp.int32)
    stacked = jnp.stack([row_block, offset, grid_row, live_flag], axis=-1)
    return stacked.reshape(TILES, 4).astype(jnp.int32)


def level_of(rng, shape, shards, least, top_value):
    gain = 1.0
    for position, shards_of in shards:
        steps = jax.random.uniform(jax.random.fold_in(jax.random.fold_in(rng, 6), position), (shards_of,), jnp.float32, least / len(shards), top_value / len(shards))
        gain = gain * jnp.repeat(jnp.exp(steps), shape[position] // shards_of).reshape((-1,) + (1,) * (len(shape) - 1 - position))
    return gain


def normal_values(key, dims, deviation, reach, shards=(), kind=jnp.bfloat16):
    gain = level_of(key, dims, shards, -0.22, 0.18) if shards else 1.0
    entries = jax.random.normal(key, dims, jnp.float32) * deviation * gain
    return jnp.minimum(jnp.maximum(entries, -reach), reach).astype(kind)


def setup_inputs(seed: int = 0) -> dict:
    streams_of = jax.random.split(jax.random.key(seed), 6)
    flux_init = normal_values(streams_of[0], (GX, HOURS, GY), 1.0, 6.0, ((0, 8), (1, 32)), jnp.float32)
    penalty = jnp.clip(jnp.exp(math.log(0.5) - 2.3025851 * jax.random.uniform(streams_of[1], (GX, HOURS, GY), jnp.float32) ** level_of(streams_of[1], (GX, HOURS, GY), ((0, 8), (1, 32)), -0.2, 0.2)), 0.05, 0.5)
    observed = normal_values(streams_of[2], (OBS,), 2.0, 12.0, ((0, 256),), jnp.float32)
    footprint = normal_values(streams_of[3], (TILES, OB, K), K ** -0.5, 0.1875, ((0, 256),))
    tile_index = draw_tile_index(jax.random.fold_in(streams_of[5], 71), 0)
    return {"flux_init": flux_init, "penalty": penalty, "observed": observed, "footprint": footprint, "tile_index": tile_index}


def laplace_of(flux):
    padded = jnp.pad(flux, 1)
    neighbours = padded[2:, 1:-1, 1:-1] + padded[:-2, 1:-1, 1:-1]
    neighbours = neighbours + padded[1:-1, 2:, 1:-1] + padded[1:-1, :-2, 1:-1]
    neighbours = neighbours + padded[1:-1, 1:-1, 2:] + padded[1:-1, 1:-1, :-2]
    return 6.0 * flux - neighbours


def reference(flux_init, penalty, observed, footprint, tile_index):
    devices_all = N_TM * N_REGION
    observed_blocks = observed.reshape(devices_all, NOB, OB)
    meta = tile_index.reshape(devices_all, NTILE, 4)
    tiles_all = footprint.reshape(devices_all, NTILE, OB, K)
    flux = flux_init
    for iteration in range(ITERS):
        flux_low = flux.astype(jnp.bfloat16)
        block_table = flux_low.reshape(GX, N_TM, K)

        def describe(device):
            info = meta[device]
            window = device // N_REGION
            panel_index = window - info[:, 1]
            usable = ((panel_index >= 0) & (info[:, 3] == 1)).astype(jnp.float32)
            return info[:, 0], info[:, 2], jnp.maximum(panel_index, 0).astype(jnp.int32), usable

        def forward(device):
            row_block, grid_row, panel_index, usable = describe(device)
            gathered = block_table[grid_row, panel_index].astype(jnp.float32)
            products = jnp.einsum('tok,tk->to', tiles_all[device].astype(jnp.float32), gathered) * usable[:, None]
            selector = (row_block[:, None] == jnp.arange(NOB, dtype=jnp.int32)[None, :]).astype(jnp.float32)
            predicted = jnp.dot(selector.T, products, precision=lax.Precision.HIGHEST)
            return (predicted - observed_blocks[device]).astype(jnp.bfloat16)

        residual = lax.map(forward, jnp.arange(devices_all, dtype=jnp.int32))

        def backward(adjoint, device):
            row_block, grid_row, panel_index, usable = describe(device)
            spread = residual[device][row_block].astype(jnp.float32)
            tile_terms = jnp.einsum('tok,to->tk', tiles_all[device].astype(jnp.float32), spread) * usable[:, None]
            target = (grid_row * N_TM + panel_index).astype(jnp.int32)
            return adjoint.at[target].add(tile_terms), None

        adjoint, unused = lax.scan(backward, jnp.zeros((GX * N_TM, K), jnp.float32), jnp.arange(devices_all, dtype=jnp.int32))
        adjoint = adjoint.reshape(GX, HOURS, GY)
        stepped = flux - 0.5 * (adjoint + 0.2 * laplace_of(flux))
        cutoff = 0.5 * penalty
        flux = stepped - jnp.clip(stepped, -cutoff, cutoff)
    return flux
```

```python
import functools

import jax
import jax.numpy as jnp
from jax import lax
from jax.experimental import pallas as pl
from jax.experimental.pallas import tpu as pltpu
from jax.sharding import PartitionSpec as P

LAG = 4
ITERS = 2
SLOTS = 48
SPREAD = 64
ROWS = 16
HOURS = 8
CELLS = 128
OBS = 128
NOB = 8
GROUP = 16
MESH = pl.DeviceIdType.MESH
HIGHEST = lax.Precision.HIGHEST


def take(ref, sem):
    pltpu.make_async_copy(ref, ref, sem).wait()


def dot(a, b, dims, precision=None):
    return lax.dot_general(
        a, b, (dims, ((), ())), precision=precision, preferred_element_type=jnp.float32
    )


def kernel(
    n_tm,
    n_region,
    tiles,
    flux_ref,
    penalty_ref,
    observed_ref,
    index_ref,
    footprint_ref,
    out_ref,
    foot,
    flux,
    low,
    window,
    blocks,
    slots,
    terms,
    all_terms,
    sums,
    parts,
    edges,
    edge_rows,
    edge_hours,
    index_pad,
    picks,
    pick,
    pick_t,
    foot_sem,
    pick_sem,
    send_sem,
    recv_sem,
    edge_send,
    edge_recv,
):
    w = lax.axis_index("tm")
    r = lax.axis_index("region")
    later = [lax.rem(w + l, n_tm) for l in range(LAG)]
    earlier = [lax.rem(w + n_tm - l, n_tm) for l in range(LAG)]
    region = [lax.rem(r + k, n_region) for k in range(n_region)]
    others = [(l, k) for l in reversed(range(LAG)) for k in range(n_region) if (l, k) != (0, 0)]
    table_rows = LAG * n_region * ROWS

    load = pltpu.make_async_copy(footprint_ref, foot, foot_sem)
    load.start()

    barrier = pltpu.get_barrier_semaphore()
    for l, k in others:
        pl.semaphore_signal(
            barrier, inc=1, device_id={"tm": earlier[l], "region": region[k]}, device_id_type=MESH
        )

    def send(src, dst, sent, received, tm, reg):
        pltpu.make_async_remote_copy(
            src_ref=src,
            dst_ref=dst,
            send_sem=sent,
            recv_sem=received,
            device_id={"tm": tm, "region": reg},
            device_id_type=MESH,
        ).start()

    index_pad[...] = jnp.zeros_like(index_pad)
    index_pad[0:4, 0:tiles] = index_ref[...]
    entries = index_pad[...]
    lag = entries[1:2, :]
    usable = (entries[3:4, :] == 1) & (lag <= w)
    mine = jnp.where(usable, lag * (n_region * ROWS) + entries[2:3, :], -1)
    picks[r] = jnp.broadcast_to(mine, (8, 128))
    for h in range(HOURS):
        flux[0, h] = flux_ref[:, h, :]
        low[0, h] = flux[0, h].astype(jnp.bfloat16)
    all_terms[...] = jnp.zeros_like(all_terms)

    pl.semaphore_wait(barrier, len(others))

    for i in range(ITERS):
        for l, k in others:
            send(
                low.at[i, region[k]],
                window.at[i, l * n_region + r],
                send_sem.at[i, 0],
                recv_sem.at[i, 0],
                later[l],
                region[k],
            )
        window[i, r] = low[i, r]
        if i == 0:
            for k in range(1, n_region):
                send(picks.at[r], picks.at[r], pick_sem.at[0], pick_sem.at[1], w, region[k])
        edges[i, 0] = flux[i, :, 0, :]
        edges[i, 1] = flux[i, :, ROWS - 1, :]
        send(
            edges.at[i, 0], edge_rows.at[i, 1],
            edge_send.at[i, 0], edge_recv.at[i, 0], w, region[n_region - 1],
        )
        send(
            edges.at[i, 1], edge_rows.at[i, 0],
            edge_send.at[i, 1], edge_recv.at[i, 1], w, region[1],
        )
        send(
            flux.at[i, HOURS - 1], edge_hours.at[i, 0],
            edge_send.at[i, 2], edge_recv.at[i, 2], later[1], r,
        )
        if i == 0:
            take(picks.at[0 : n_region - 1], pick_sem.at[1])
            rows = picks[:, 0, :]
            columns = jnp.transpose(jnp.concatenate([rows] * 16, axis=0))
            across = lax.broadcasted_iota(jnp.int32, (SLOTS, table_rows), 1)
            for d in range(n_region):
                chosen = columns[0:SLOTS, d : d + 1] == across
                pick[d * SLOTS : (d + 1) * SLOTS, :] = chosen.astype(jnp.float32).astype(jnp.bfloat16)
            lane = lax.broadcasted_iota(jnp.int32, (1, 128), 1)
            moved = pltpu.roll(rows, SPREAD, 1)
            down = lax.broadcasted_iota(jnp.int32, (table_rows, 128), 0)
            for d in range(0, n_region, 2):
                pair = jnp.where(lane < SPREAD, rows[d : d + 1], moved[d + 1 : d + 2])
                chosen = down == pair
                pick_t[:, d * SPREAD : (d + 2) * SPREAD] = chosen.astype(jnp.float32).astype(
                    jnp.bfloat16
                )
        take(window.at[i, 0 : len(others)], recv_sem.at[i, 0])
        send(
            flux.at[i, 0], edge_hours.at[i, 1],
            edge_send.at[i, 3], edge_recv.at[i, 3], earlier[1], r,
        )

        table = window[i].reshape(table_rows, CELLS)
        blocks[i] = (
            dot(pick[...], table, ((1,), (0,)))
            .astype(jnp.bfloat16)
            .reshape(n_region, SLOTS, CELLS)
        )
        for k in range(1, n_region):
            send(
                blocks.at[i, region[k]], slots.at[i, r],
                send_sem.at[i, 1], recv_sem.at[i, 1], w, region[k],
            )
        slots[i, r] = blocks[i, r]
        if i == 0:
            load.wait()
        take(slots.at[i, 0 : n_region - 1], recv_sem.at[i, 1])

        down = lax.broadcasted_iota(jnp.int32, (GROUP, OBS), 0)
        x = jnp.concatenate([slots[i, h] for h in range(HOURS)], axis=1)
        products = []
        for first in range(0, SLOTS, GROUP):
            x_group = x[first : first + GROUP, :]
            total = jnp.zeros((GROUP, OBS), jnp.float32)
            for t in range(first, min(first + GROUP, tiles), 2):
                both = dot(x_group, foot[t * OBS : (t + 2) * OBS, :], ((1,), (1,)))
                total = jnp.where(down == t - first, both[:, :OBS], total)
                total = jnp.where(down == t + 1 - first, both[:, OBS:], total)
            products.append(total)
        products = jnp.concatenate(products, axis=0)
        row_block = index_pad[0:1, 0:SLOTS]
        selector = (lax.broadcasted_iota(jnp.int32, (NOB, SLOTS), 0) == row_block).astype(jnp.float32)
        predicted = dot(selector, products, ((1,), (0,)), HIGHEST)
        residual = (predicted - observed_ref[...]).astype(jnp.bfloat16).astype(jnp.float32)

        spread = jnp.zeros((SLOTS, OBS), jnp.float32)
        block_of = jnp.transpose(index_pad[...])[0:SLOTS, 0:1]
        for b in range(NOB):
            spread = jnp.where(block_of == b, residual[b : b + 1, :], spread)
        lefts = []
        for first in range(0, SLOTS, GROUP):
            part = spread[first : first + GROUP, :]
            lefts.append(
                jnp.concatenate(
                    [
                        jnp.where(down == t - first, part, 0.0)
                        for t in range(first, min(first + GROUP, tiles))
                    ],
                    axis=1,
                ).astype(jnp.bfloat16)
            )
        for h in range(0, HOURS, 2):
            for g, first in enumerate(range(0, SLOTS, GROUP)):
                last = min(first + GROUP, tiles)
                both = dot(
                    lefts[g],
                    foot[first * OBS : last * OBS, h * CELLS : (h + 2) * CELLS],
                    ((1,), (0,)),
                ).astype(jnp.bfloat16)
                terms[i, h, first : first + GROUP, :] = both[:, :CELLS]
                terms[i, h + 1, first : first + GROUP, :] = both[:, CELLS:]
        for k in range(1, n_region):
            send(
                terms.at[i, region[k]], all_terms.at[i, r, 0:SLOTS],
                send_sem.at[i, 2], recv_sem.at[i, 2], w, region[k],
            )
        all_terms[i, r, 0:SLOTS] = terms[i, r]
        take(all_terms.at[i, 0 : n_region - 1, 0:SLOTS], recv_sem.at[i, 2])

        received = all_terms[i].reshape(n_region * SPREAD, CELLS)
        sums[i] = (
            dot(pick_t[...], received, ((1,), (0,)))
            .astype(jnp.bfloat16)
            .reshape(LAG * n_region, ROWS, CELLS)
        )
        for l, k in others:
            send(
                sums.at[i, l * n_region + region[k]],
                parts.at[i, l * n_region + r],
                send_sem.at[i, 3],
                recv_sem.at[i, 3],
                earlier[l],
                region[k],
            )
        parts[i, r] = sums[i, r]
        for e in range(2):
            take(edge_rows.at[i, e], edge_recv.at[i, e])
            take(edge_hours.at[i, e], edge_recv.at[i, 2 + e])
        take(parts.at[i, 0 : len(others)], recv_sem.at[i, 3])

        row_low = jnp.where(r > 0, edge_rows[i, 0], 0.0)
        row_high = jnp.where(r < n_region - 1, edge_rows[i, 1], 0.0)
        hour_low = jnp.where(w > 0, edge_hours[i, 0], 0.0)
        hour_high = jnp.where(w < n_tm - 1, edge_hours[i, 1], 0.0)
        cell = lax.broadcasted_iota(jnp.int32, (ROWS, CELLS), 1)
        planes = [hour_low] + [flux[i, h] for h in range(HOURS)] + [hour_high]
        for h in range(HOURS):
            here = planes[h + 1]
            adjoint = parts[i, h].astype(jnp.float32)
            for l in range(1, LAG):
                adjoint = adjoint + parts[i, l * n_region + h].astype(jnp.float32)
            neighbours = jnp.concatenate([here[1:], row_high[h : h + 1]], axis=0)
            neighbours = neighbours + jnp.concatenate([row_low[h : h + 1], here[:-1]], axis=0)
            neighbours = neighbours + planes[h + 2] + planes[h]
            neighbours = neighbours + jnp.where(cell < CELLS - 1, pltpu.roll(here, CELLS - 1, 1), 0.0)
            neighbours = neighbours + jnp.where(cell > 0, pltpu.roll(here, 1, 1), 0.0)
            laplace = 6.0 * here - neighbours
            stepped = here - 0.5 * (adjoint + 0.2 * laplace)
            cutoff = 0.5 * penalty_ref[:, h, :]
            new = stepped - jnp.clip(stepped, -cutoff, cutoff)
            if i < ITERS - 1:
                flux[i + 1, h] = new
                low[i + 1, h] = new.astype(jnp.bfloat16)
            else:
                out_ref[:, h, :] = new

    take(picks.at[0 : n_region - 1], pick_sem.at[0])
    for i in range(ITERS):
        take(window.at[i, 0 : len(others)], send_sem.at[i, 0])
        take(slots.at[i, 0 : n_region - 1], send_sem.at[i, 1])
        take(terms.at[i, 0 : n_region - 1], send_sem.at[i, 2])
        take(parts.at[i, 0 : len(others)], send_sem.at[i, 3])
        for e in range(2):
            take(edge_rows.at[i, e], edge_send.at[i, e])
            take(edge_hours.at[i, e], edge_send.at[i, 2 + e])


def local(flux_init, penalty, observed, footprint, tile_index):
    n_tm, n_region = lax.axis_size("tm"), lax.axis_size("region")
    tiles = tile_index.shape[0]
    in_vmem = pl.BlockSpec(memory_space=pltpu.VMEM)
    table = LAG * n_region
    half, full = jnp.bfloat16, jnp.float32
    dma = pltpu.SemaphoreType.DMA
    return pl.pallas_call(
        functools.partial(kernel, n_tm, n_region, tiles),
        out_shape=jax.ShapeDtypeStruct(flux_init.shape, full),
        in_specs=[in_vmem] * 4 + [pl.BlockSpec(memory_space=pl.ANY)],
        out_specs=in_vmem,
        scratch_shapes=[
            pltpu.VMEM((tiles * OBS, HOURS * CELLS), half),
            pltpu.VMEM((ITERS, HOURS, ROWS, CELLS), full),
            pltpu.VMEM((ITERS, HOURS, ROWS, CELLS), half),
            pltpu.VMEM((ITERS, table, ROWS, CELLS), half),
            pltpu.VMEM((ITERS, n_region, SLOTS, CELLS), half),
            pltpu.VMEM((ITERS, n_region, SLOTS, CELLS), half),
            pltpu.VMEM((ITERS, n_region, SLOTS, CELLS), half),
            pltpu.VMEM((ITERS, n_region, SPREAD, CELLS), half),
            pltpu.VMEM((ITERS, table, ROWS, CELLS), half),
            pltpu.VMEM((ITERS, table, ROWS, CELLS), half),
            pltpu.VMEM((ITERS, 2, HOURS, CELLS), full),
            pltpu.VMEM((ITERS, 2, HOURS, CELLS), full),
            pltpu.VMEM((ITERS, 2, ROWS, CELLS), full),
            pltpu.VMEM((128, 128), jnp.int32),
            pltpu.VMEM((n_region, 8, 128), jnp.int32),
            pltpu.VMEM((n_region * SLOTS, table * ROWS), half),
            pltpu.VMEM((table * ROWS, n_region * SPREAD), half),
            dma,
            dma((2,)),
            dma((ITERS, 4)),
            dma((ITERS, 4)),
            dma((ITERS, 4)),
            dma((ITERS, 4)),
        ],
        compiler_params=pltpu.CompilerParams(
            collective_id=0, has_side_effects=True, vmem_limit_bytes=60 * 2**20
        ),
        cost_estimate=pl.CostEstimate(
            flops=8 * footprint.size, bytes_accessed=2 * footprint.size, transcendentals=0
        ),
    )(
        flux_init,
        penalty,
        observed.reshape(NOB, OBS),
        tile_index.T,
        footprint.reshape(tiles * OBS, HOURS * CELLS),
    )


def solution(mesh):
    in_specs = (
        P("region", "tm", None),
        P("region", "tm", None),
        P(("tm", "region")),
        P(("tm", "region"), None, None),
        P(("tm", "region"), None),
    )
    out_specs = P("region", "tm", None)
    return jax.shard_map(local, mesh=mesh, in_specs=in_specs, out_specs=out_specs, check_vma=False)
```

```python
import functools

import jax
import jax.numpy as jnp
from jax import lax
from jax.experimental import pallas as pl
from jax.experimental.pallas import tpu as pltpu
from jax.sharding import PartitionSpec as P

LAG = 4
ITERS = 2
SLOTS = 48
SPREAD = 64
ROWS = 16
HOURS = 8
CELLS = 128
OBS = 128
NOB = 8
GROUP = 16
MESH = pl.DeviceIdType.MESH
HIGHEST = lax.Precision.HIGHEST


def take(ref, sem):
    pltpu.make_async_copy(ref, ref, sem).wait()


def dot(a, b, dims, precision=None):
    return lax.dot_general(
        a, b, (dims, ((), ())), precision=precision, preferred_element_type=jnp.float32
    )


def kernel(
    n_tm,
    n_region,
    tiles,
    flux_ref,
    penalty_ref,
    observed_ref,
    index_ref,
    footprint_ref,
    out_ref,
    foot,
    foot_t,
    flux,
    low,
    window,
    blocks,
    slots,
    terms,
    all_terms,
    sums,
    parts,
    edges,
    edge_rows,
    edge_hours,
    index_pad,
    picks,
    pick,
    pick_t,
    foot_sem,
    pick_sem,
    send_sem,
    recv_sem,
    slot_recv,
    edge_send,
    edge_recv,
):
    w = lax.axis_index("tm")
    r = lax.axis_index("region")
    later = [lax.rem(w + l, n_tm) for l in range(LAG)]
    earlier = [lax.rem(w + n_tm - l, n_tm) for l in range(LAG)]
    region = [lax.rem(r + k, n_region) for k in range(n_region)]
    others = [(l, k) for l in reversed(range(LAG)) for k in range(n_region) if (l, k) != (0, 0)]
    table_rows = LAG * n_region * ROWS
    own = r // 2
    flip = own + 1 - 2 * lax.rem(own, 2)
    pairs = [own, flip, lax.rem(own + 2, 4), lax.rem(flip + 2, 4)]
    partner = r + 1 - 2 * lax.rem(r, 2)
    near_first = [partner] + [2 * q + e for q in pairs[1:] for e in range(2)]

    load = pltpu.make_async_copy(footprint_ref, foot, foot_sem)
    load.start()

    barrier = pltpu.get_barrier_semaphore()
    for l, k in others:
        pl.semaphore_signal(
            barrier, inc=1, device_id={"tm": earlier[l], "region": region[k]}, device_id_type=MESH
        )

    def send(src, dst, sent, received, tm, reg):
        pltpu.make_async_remote_copy(
            src_ref=src,
            dst_ref=dst,
            send_sem=sent,
            recv_sem=received,
            device_id={"tm": tm, "region": reg},
            device_id_type=MESH,
        ).start()

    index_pad[...] = jnp.zeros_like(index_pad)
    index_pad[0:4, 0:tiles] = index_ref[...]
    entries = index_pad[...]
    lag = entries[1:2, :]
    usable = (entries[3:4, :] == 1) & (lag <= w)
    mine = jnp.where(usable, lag * (n_region * ROWS) + entries[2:3, :], -1)
    picks[r] = jnp.broadcast_to(mine, (8, 128))
    for h in range(HOURS):
        flux[0, h] = flux_ref[:, h, :]
        low[0, h] = flux[0, h].astype(jnp.bfloat16)
    all_terms[...] = jnp.zeros_like(all_terms)

    pl.semaphore_wait(barrier, len(others))

    for i in range(ITERS):
        for l, k in others:
            send(
                low.at[i, region[k]],
                window.at[i, l * n_region + r],
                send_sem.at[i, 0],
                recv_sem.at[i, 0],
                later[l],
                region[k],
            )
        window[i, r] = low[i, r]
        if i == 0:
            for k in range(1, n_region):
                send(picks.at[r], picks.at[r], pick_sem.at[0], pick_sem.at[1], w, region[k])
        edges[i, 0] = flux[i, :, 0, :]
        edges[i, 1] = flux[i, :, ROWS - 1, :]
        send(
            edges.at[i, 0], edge_rows.at[i, 1],
            edge_send.at[i, 0], edge_recv.at[i, 0], w, region[n_region - 1],
        )
        send(
            edges.at[i, 1], edge_rows.at[i, 0],
            edge_send.at[i, 1], edge_recv.at[i, 1], w, region[1],
        )
        send(
            flux.at[i, HOURS - 1], edge_hours.at[i, 0],
            edge_send.at[i, 2], edge_recv.at[i, 2], later[1], r,
        )
        if i == 0:
            load.wait()
            for t in range(tiles):
                foot_t[:, t * OBS : (t + 1) * OBS] = jnp.transpose(foot[t * OBS : (t + 1) * OBS, :])
            take(picks.at[0 : n_region - 1], pick_sem.at[1])
            rows = picks[:, 0, :]
            columns = jnp.transpose(jnp.concatenate([rows] * 16, axis=0))
            across = lax.broadcasted_iota(jnp.int32, (SLOTS, table_rows), 1)
            for d in range(n_region):
                chosen = columns[0:SLOTS, d : d + 1] == across
                pick[d * SLOTS : (d + 1) * SLOTS, :] = chosen.astype(jnp.float32).astype(jnp.bfloat16)
            lane = lax.broadcasted_iota(jnp.int32, (1, 128), 1)
            moved = pltpu.roll(rows, SPREAD, 1)
            down = lax.broadcasted_iota(jnp.int32, (table_rows, 128), 0)
            for d in range(0, n_region, 2):
                pair = jnp.where(lane < SPREAD, rows[d : d + 1], moved[d + 1 : d + 2])
                chosen = down == pair
                pick_t[:, d * SPREAD : (d + 2) * SPREAD] = chosen.astype(jnp.float32).astype(
                    jnp.bfloat16
                )
        take(window.at[i, 0 : len(others)], recv_sem.at[i, 0])
        send(
            flux.at[i, 0], edge_hours.at[i, 1],
            edge_send.at[i, 3], edge_recv.at[i, 3], earlier[1], r,
        )

        table = window[i].reshape(table_rows, CELLS)
        blocks[i] = (
            dot(pick[...], table, ((1,), (0,)))
            .astype(jnp.bfloat16)
            .reshape(n_region, SLOTS, CELLS)
        )
        for reg in reversed(near_first):
            send(
                blocks.at[i, reg], slots.at[i, r],
                send_sem.at[i, 1], slot_recv.at[i, r], w, reg,
            )
        slots[i, r] = blocks[i, r]

        down = lax.broadcasted_iota(jnp.int32, (GROUP, OBS), 0)
        groups = [(first, min(first + GROUP, tiles)) for first in range(0, SLOTS, GROUP)]
        products = [jnp.zeros((GROUP, OBS), jnp.float32) for _ in groups]
        for step, q in enumerate(pairs):
            for reg in [2 * q, 2 * q + 1] if step else [partner]:
                take(slots.at[i, reg], slot_recv.at[i, reg])
            x = jnp.concatenate([slots[i, 2 * q], slots[i, 2 * q + 1]], axis=1)
            cells = pl.ds(pl.multiple_of(q * 2 * CELLS, 2 * CELLS), 2 * CELLS)
            for g, (first, last) in enumerate(groups):
                x_group = x[first : first + GROUP, :]
                total = jnp.zeros((GROUP, OBS), jnp.float32)
                for t in range(first, last, 2):
                    both = dot(x_group, foot_t[cells, t * OBS : (t + 2) * OBS], ((1,), (0,)))
                    total = jnp.where(down == t - first, both[:, :OBS], total)
                    total = jnp.where(down == t + 1 - first, both[:, OBS:], total)
                products[g] = products[g] + total
        products = jnp.concatenate(products, axis=0)
        row_block = index_pad[0:1, 0:SLOTS]
        selector = (lax.broadcasted_iota(jnp.int32, (NOB, SLOTS), 0) == row_block).astype(jnp.float32)
        predicted = dot(selector, products, ((1,), (0,)), HIGHEST)
        residual = (predicted - observed_ref[...]).astype(jnp.bfloat16).astype(jnp.float32)

        spread = jnp.zeros((SLOTS, OBS), jnp.float32)
        block_of = jnp.transpose(index_pad[...])[0:SLOTS, 0:1]
        for b in range(NOB):
            spread = jnp.where(block_of == b, residual[b : b + 1, :], spread)
        lefts = []
        for first in range(0, SLOTS, GROUP):
            part = spread[first : first + GROUP, :]
            lefts.append(
                jnp.concatenate(
                    [
                        jnp.where(down == t - first, part, 0.0)
                        for t in range(first, min(first + GROUP, tiles))
                    ],
                    axis=1,
                ).astype(jnp.bfloat16)
            )
        for q in reversed(pairs):
            cells = pl.ds(pl.multiple_of(q * 2 * CELLS, 2 * CELLS), 2 * CELLS)
            for g, (first, last) in enumerate(groups):
                both = dot(
                    lefts[g], foot[first * OBS : last * OBS, cells], ((1,), (0,))
                ).astype(jnp.bfloat16)
                terms[i, 2 * q, first : first + GROUP, :] = both[:, :CELLS]
                terms[i, 2 * q + 1, first : first + GROUP, :] = both[:, CELLS:]
            for reg in [2 * q, 2 * q + 1] if q is not own else [partner]:
                send(
                    terms.at[i, reg], all_terms.at[i, r, 0:SLOTS],
                    send_sem.at[i, 2], recv_sem.at[i, 2], w, reg,
                )
        all_terms[i, r, 0:SLOTS] = terms[i, r]
        take(all_terms.at[i, 0 : n_region - 1, 0:SLOTS], recv_sem.at[i, 2])

        received = all_terms[i].reshape(n_region * SPREAD, CELLS)
        sums[i] = (
            dot(pick_t[...], received, ((1,), (0,)))
            .astype(jnp.bfloat16)
            .reshape(LAG * n_region, ROWS, CELLS)
        )
        for l, k in others:
            send(
                sums.at[i, l * n_region + region[k]],
                parts.at[i, l * n_region + r],
                send_sem.at[i, 3],
                recv_sem.at[i, 3],
                earlier[l],
                region[k],
            )
        parts[i, r] = sums[i, r]
        for e in range(2):
            take(edge_rows.at[i, e], edge_recv.at[i, e])
            take(edge_hours.at[i, e], edge_recv.at[i, 2 + e])
        take(parts.at[i, 0 : len(others)], recv_sem.at[i, 3])

        row_low = jnp.where(r > 0, edge_rows[i, 0], 0.0)
        row_high = jnp.where(r < n_region - 1, edge_rows[i, 1], 0.0)
        hour_low = jnp.where(w > 0, edge_hours[i, 0], 0.0)
        hour_high = jnp.where(w < n_tm - 1, edge_hours[i, 1], 0.0)
        cell = lax.broadcasted_iota(jnp.int32, (ROWS, CELLS), 1)
        planes = [hour_low] + [flux[i, h] for h in range(HOURS)] + [hour_high]
        for h in range(HOURS):
            here = planes[h + 1]
            adjoint = parts[i, h].astype(jnp.float32)
            for l in range(1, LAG):
                adjoint = adjoint + parts[i, l * n_region + h].astype(jnp.float32)
            neighbours = jnp.concatenate([here[1:], row_high[h : h + 1]], axis=0)
            neighbours = neighbours + jnp.concatenate([row_low[h : h + 1], here[:-1]], axis=0)
            neighbours = neighbours + planes[h + 2] + planes[h]
            neighbours = neighbours + jnp.where(cell < CELLS - 1, pltpu.roll(here, CELLS - 1, 1), 0.0)
            neighbours = neighbours + jnp.where(cell > 0, pltpu.roll(here, 1, 1), 0.0)
            laplace = 6.0 * here - neighbours
            stepped = here - 0.5 * (adjoint + 0.2 * laplace)
            cutoff = 0.5 * penalty_ref[:, h, :]
            new = stepped - jnp.clip(stepped, -cutoff, cutoff)
            if i < ITERS - 1:
                flux[i + 1, h] = new
                low[i + 1, h] = new.astype(jnp.bfloat16)
            else:
                out_ref[:, h, :] = new

    take(picks.at[0 : n_region - 1], pick_sem.at[0])
    for i in range(ITERS):
        take(window.at[i, 0 : len(others)], send_sem.at[i, 0])
        take(slots.at[i, 0 : n_region - 1], send_sem.at[i, 1])
        take(terms.at[i, 0 : n_region - 1], send_sem.at[i, 2])
        take(parts.at[i, 0 : len(others)], send_sem.at[i, 3])
        for e in range(2):
            take(edge_rows.at[i, e], edge_send.at[i, e])
            take(edge_hours.at[i, e], edge_send.at[i, 2 + e])


def local(flux_init, penalty, observed, footprint, tile_index):
    n_tm, n_region = lax.axis_size("tm"), lax.axis_size("region")
    tiles = tile_index.shape[0]
    in_vmem = pl.BlockSpec(memory_space=pltpu.VMEM)
    table = LAG * n_region
    half, full = jnp.bfloat16, jnp.float32
    dma = pltpu.SemaphoreType.DMA
    return pl.pallas_call(
        functools.partial(kernel, n_tm, n_region, tiles),
        out_shape=jax.ShapeDtypeStruct(flux_init.shape, full),
        in_specs=[in_vmem] * 4 + [pl.BlockSpec(memory_space=pl.ANY)],
        out_specs=in_vmem,
        scratch_shapes=[
            pltpu.VMEM((tiles * OBS, HOURS * CELLS), half),
            pltpu.VMEM((HOURS * CELLS, tiles * OBS), half),
            pltpu.VMEM((ITERS, HOURS, ROWS, CELLS), full),
            pltpu.VMEM((ITERS, HOURS, ROWS, CELLS), half),
            pltpu.VMEM((ITERS, table, ROWS, CELLS), half),
            pltpu.VMEM((ITERS, n_region, SLOTS, CELLS), half),
            pltpu.VMEM((ITERS, n_region, SLOTS, CELLS), half),
            pltpu.VMEM((ITERS, n_region, SLOTS, CELLS), half),
            pltpu.VMEM((ITERS, n_region, SPREAD, CELLS), half),
            pltpu.VMEM((ITERS, table, ROWS, CELLS), half),
            pltpu.VMEM((ITERS, table, ROWS, CELLS), half),
            pltpu.VMEM((ITERS, 2, HOURS, CELLS), full),
            pltpu.VMEM((ITERS, 2, HOURS, CELLS), full),
            pltpu.VMEM((ITERS, 2, ROWS, CELLS), full),
            pltpu.VMEM((128, 128), jnp.int32),
            pltpu.VMEM((n_region, 8, 128), jnp.int32),
            pltpu.VMEM((n_region * SLOTS, table * ROWS), half),
            pltpu.VMEM((table * ROWS, n_region * SPREAD), half),
            dma,
            dma((2,)),
            dma((ITERS, 4)),
            dma((ITERS, 4)),
            dma((ITERS, n_region)),
            dma((ITERS, 4)),
            dma((ITERS, 4)),
        ],
        compiler_params=pltpu.CompilerParams(
            collective_id=0, has_side_effects=True, vmem_limit_bytes=55 * 2**20
        ),
        cost_estimate=pl.CostEstimate(
            flops=8 * footprint.size, bytes_accessed=2 * footprint.size, transcendentals=0
        ),
    )(
        flux_init,
        penalty,
        observed.reshape(NOB, OBS),
        tile_index.T,
        footprint.reshape(tiles * OBS, HOURS * CELLS),
    )


def solution(mesh):
    in_specs = (
        P("region", "tm", None),
        P("region", "tm", None),
        P(("tm", "region")),
        P(("tm", "region"), None, None),
        P(("tm", "region"), None),
    )
    out_specs = P("region", "tm", None)
    return jax.shard_map(local, mesh=mesh, in_specs=in_specs, out_specs=out_specs, check_vma=False)
```

```python
import functools

import jax
import jax.numpy as jnp
from jax import lax
from jax.experimental import pallas as pl
from jax.experimental.pallas import tpu as pltpu
from jax.sharding import PartitionSpec as P

LAG = 4
ITERS = 2
SLOTS = 48
SPREAD = 64
ROWS = 16
HOURS = 8
CELLS = 128
OBS = 128
NOB = 8
GROUP = 16
MESH = pl.DeviceIdType.MESH
HIGHEST = lax.Precision.HIGHEST


def take(ref, sem):
    pltpu.make_async_copy(ref, ref, sem).wait()


def dot(a, b, dims, precision=None):
    return lax.dot_general(
        a, b, (dims, ((), ())), precision=precision, preferred_element_type=jnp.float32
    )


def kernel(
    n_tm,
    n_region,
    tiles,
    flux_hbm,
    penalty_hbm,
    observed_hbm,
    index_hbm,
    footprint_ref,
    out_ref,
    flux_ref,
    penalty_ref,
    observed_ref,
    index_ref,
    foot,
    foot_t,
    flux,
    low,
    window,
    blocks,
    slots,
    terms,
    all_terms,
    sums,
    parts,
    base,
    owned,
    fields,
    nearby,
    whole_out,
    whole_in,
    edges,
    edge_rows,
    edge_hours,
    index_pad,
    picks,
    pick,
    pick_t,
    foot_sem,
    input_sem,
    pick_sem,
    send_sem,
    recv_sem,
    slot_recv,
    side_sem,
    edge_send,
    edge_recv,
):
    w = lax.axis_index("tm")
    r = lax.axis_index("region")
    later = [lax.rem(w + l, n_tm) for l in range(LAG)]
    earlier = [lax.rem(w + n_tm - l, n_tm) for l in range(LAG)]
    region = [lax.rem(r + k, n_region) for k in range(n_region)]
    others = [(l, k) for l in reversed(range(LAG)) for k in range(n_region) if (l, k) != (0, 0)]
    table_rows = LAG * n_region * ROWS
    own = r // 2
    flip = own + 1 - 2 * lax.rem(own, 2)
    pairs = [own, flip, lax.rem(own + 2, 4), lax.rem(flip + 2, 4)]
    partner = r + 1 - 2 * lax.rem(r, 2)
    near_first = [partner] + [2 * q + e for q in pairs[1:] for e in range(2)]

    barrier = pltpu.get_barrier_semaphore()
    for l, k in others:
        pl.semaphore_signal(
            barrier, inc=1, device_id={"tm": earlier[l], "region": region[k]}, device_id_type=MESH
        )
    pl.semaphore_signal(barrier, inc=1, device_id={"tm": later[1], "region": r}, device_id_type=MESH)

    inputs = [
        pltpu.make_async_copy(src, dst, input_sem.at[k])
        for k, (src, dst) in enumerate(
            [
                (flux_hbm, flux_ref),
                (index_hbm, index_ref),
                (observed_hbm, observed_ref),
                (penalty_hbm, penalty_ref),
            ]
        )
    ]
    load = pltpu.make_async_copy(footprint_ref, foot, foot_sem)
    for copy in inputs + [load]:
        copy.start()

    def send(src, dst, sent, received, tm, reg):
        pltpu.make_async_remote_copy(
            src_ref=src,
            dst_ref=dst,
            send_sem=sent,
            recv_sem=received,
            device_id={"tm": tm, "region": reg},
            device_id_type=MESH,
        ).start()

    index_pad[...] = jnp.zeros_like(index_pad)
    all_terms[...] = jnp.zeros_like(all_terms)
    for copy in inputs:
        copy.wait()
    index_pad[0:4, 0:tiles] = index_ref[...]
    entries = index_pad[...]
    lag = entries[1:2, :]
    usable = (entries[3:4, :] == 1) & (lag <= w)
    mine = jnp.where(usable, lag * (n_region * ROWS) + entries[2:3, :], -1)
    picks[r] = jnp.broadcast_to(mine, (8, 128))
    for h in range(HOURS):
        flux[0, h] = flux_ref[:, h, :]
        low[h] = flux[0, h].astype(jnp.bfloat16)

    pl.semaphore_wait(barrier, len(others) + 1)

    def send_edges(i):
        edges[i, 0] = flux[i, :, 0, :]
        edges[i, 1] = flux[i, :, ROWS - 1, :]
        for e, (src, dst, tm, reg) in enumerate(
            [
                (edges.at[i, 1], edge_rows.at[i, 0], w, region[1]),
                (edges.at[i, 0], edge_rows.at[i, 1], w, region[n_region - 1]),
                (flux.at[i, HOURS - 1], edge_hours.at[i, 0], later[1], r),
                (flux.at[i, 0], edge_hours.at[i, 1], earlier[1], r),
            ]
        ):
            send(src, dst, edge_send.at[i, e], edge_recv.at[i, e], tm, reg)

    def make_base(i):
        for e in range(2):
            take(edge_rows.at[i, e], edge_recv.at[i, e])
            take(edge_hours.at[i, e], edge_recv.at[i, 2 + e])
        row_low = jnp.where(r > 0, edge_rows[i, 0], 0.0)
        row_high = jnp.where(r < n_region - 1, edge_rows[i, 1], 0.0)
        hour_low = jnp.where(w > 0, edge_hours[i, 0], 0.0)
        hour_high = jnp.where(w < n_tm - 1, edge_hours[i, 1], 0.0)
        cell = lax.broadcasted_iota(jnp.int32, (ROWS, CELLS), 1)
        planes = [hour_low] + [flux[i, h] for h in range(HOURS)] + [hour_high]
        for h in range(HOURS):
            here = planes[h + 1]
            neighbours = jnp.concatenate([here[1:], row_high[h : h + 1]], axis=0)
            neighbours = neighbours + jnp.concatenate([row_low[h : h + 1], here[:-1]], axis=0)
            neighbours = neighbours + planes[h + 2] + planes[h]
            neighbours = neighbours + jnp.where(cell < CELLS - 1, pltpu.roll(here, CELLS - 1, 1), 0.0)
            neighbours = neighbours + jnp.where(cell > 0, pltpu.roll(here, 1, 1), 0.0)
            base[i, h] = here - 0.1 * (6.0 * here - neighbours)

    def stepped(start, adjoint, cutoff):
        value = start - 0.5 * adjoint
        return value - jnp.clip(value, -cutoff, cutoff)

    for i in range(ITERS):
        if i == 0:
            for l, k in others:
                send(
                    low.at[region[k]], window.at[0, l * n_region + r],
                    send_sem.at[0, 0], recv_sem.at[0, 0], later[l], region[k],
                )
            window[0, r] = low[r]
            for k in range(1, n_region):
                send(picks.at[r], picks.at[r], pick_sem.at[0], pick_sem.at[1], w, region[k])
            send_edges(0)
        if i == 0:
            load.wait()
            for t in range(tiles):
                foot_t[:, t * OBS : (t + 1) * OBS] = jnp.transpose(foot[t * OBS : (t + 1) * OBS, :])
            take(picks.at[0 : n_region - 1], pick_sem.at[1])
            rows = picks[:, 0, :]
            columns = jnp.transpose(jnp.concatenate([rows] * 16, axis=0))
            across = lax.broadcasted_iota(jnp.int32, (SLOTS, table_rows), 1)
            for d in range(n_region):
                chosen = columns[0:SLOTS, d : d + 1] == across
                pick[d * SLOTS : (d + 1) * SLOTS, :] = chosen.astype(jnp.float32).astype(jnp.bfloat16)
            lane = lax.broadcasted_iota(jnp.int32, (1, 128), 1)
            moved = pltpu.roll(rows, SPREAD, 1)
            down = lax.broadcasted_iota(jnp.int32, (table_rows, 128), 0)
            for d in range(0, n_region, 2):
                pair = jnp.where(lane < SPREAD, rows[d : d + 1], moved[d + 1 : d + 2])
                chosen = down == pair
                pick_t[:, d * SPREAD : (d + 2) * SPREAD] = chosen.astype(jnp.float32).astype(
                    jnp.bfloat16
                )
            make_base(0)
            for h in range(HOURS):
                owned[h, 0] = base[0, h].astype(jnp.bfloat16)
                owned[h, 1] = (0.5 * penalty_ref[:, h, :]).astype(jnp.bfloat16)
            take(window.at[0, 0 : len(others)], recv_sem.at[0, 0])

        table = window[i].reshape(table_rows, CELLS)
        blocks[i] = (
            dot(pick[...], table, ((1,), (0,)))
            .astype(jnp.bfloat16)
            .reshape(n_region, SLOTS, CELLS)
        )
        for reg in reversed(near_first):
            send(
                blocks.at[i, reg], slots.at[i, r],
                send_sem.at[i, 1], slot_recv.at[i, r], w, reg,
            )
        slots[i, r] = blocks[i, r]
        if i == 0:
            for l, k in others:
                send(
                    owned.at[region[k]], fields.at[l * n_region + r],
                    side_sem.at[0, 0], side_sem.at[0, 1], later[l], region[k],
                )
            fields[r] = owned[r]
        else:
            for reg in reversed(near_first):
                send(whole_out.at[reg], whole_in.at[r], side_sem.at[1, 0], side_sem.at[1, 1], w, reg)
            whole_in[r] = whole_out[r]

        down = lax.broadcasted_iota(jnp.int32, (GROUP, OBS), 0)
        groups = [(first, min(first + GROUP, tiles)) for first in range(0, SLOTS, GROUP)]
        products = [jnp.zeros((GROUP, OBS), jnp.float32) for _ in groups]
        for step, q in enumerate(pairs):
            for reg in [2 * q, 2 * q + 1] if step else [partner]:
                take(slots.at[i, reg], slot_recv.at[i, reg])
            x = jnp.concatenate([slots[i, 2 * q], slots[i, 2 * q + 1]], axis=1)
            cells = pl.ds(pl.multiple_of(q * 2 * CELLS, 2 * CELLS), 2 * CELLS)
            for g, (first, last) in enumerate(groups):
                x_group = x[first : first + GROUP, :]
                total = jnp.zeros((GROUP, OBS), jnp.float32)
                for t in range(first, last, 2):
                    both = dot(x_group, foot_t[cells, t * OBS : (t + 2) * OBS], ((1,), (0,)))
                    total = jnp.where(down == t - first, both[:, :OBS], total)
                    total = jnp.where(down == t + 1 - first, both[:, OBS:], total)
                products[g] = products[g] + total
        products = jnp.concatenate(products, axis=0)
        row_block = index_pad[0:1, 0:SLOTS]
        selector = (lax.broadcasted_iota(jnp.int32, (NOB, SLOTS), 0) == row_block).astype(jnp.float32)
        predicted = dot(selector, products, ((1,), (0,)), HIGHEST)
        residual = (predicted - observed_ref[...]).astype(jnp.bfloat16).astype(jnp.float32)

        spread = jnp.zeros((SLOTS, OBS), jnp.float32)
        block_of = jnp.transpose(index_pad[...])[0:SLOTS, 0:1]
        for b in range(NOB):
            spread = jnp.where(block_of == b, residual[b : b + 1, :], spread)
        lefts = []
        for first in range(0, SLOTS, GROUP):
            part = spread[first : first + GROUP, :]
            lefts.append(
                jnp.concatenate(
                    [
                        jnp.where(down == t - first, part, 0.0)
                        for t in range(first, min(first + GROUP, tiles))
                    ],
                    axis=1,
                ).astype(jnp.bfloat16)
            )
        for q in reversed(pairs):
            cells = pl.ds(pl.multiple_of(q * 2 * CELLS, 2 * CELLS), 2 * CELLS)
            for g, (first, last) in enumerate(groups):
                both = dot(
                    lefts[g], foot[first * OBS : last * OBS, cells], ((1,), (0,))
                ).astype(jnp.bfloat16)
                terms[i, 2 * q, first : first + GROUP, :] = both[:, :CELLS]
                terms[i, 2 * q + 1, first : first + GROUP, :] = both[:, CELLS:]
            for reg in [2 * q, 2 * q + 1] if q is not own else [partner]:
                send(
                    terms.at[i, reg], all_terms.at[i, r, 0:SLOTS],
                    send_sem.at[i, 2], recv_sem.at[i, 2], w, reg,
                )
        all_terms[i, r, 0:SLOTS] = terms[i, r]
        if i > 0:
            take(whole_in.at[0 : n_region - 1], side_sem.at[1, 1])
            for h in range(HOURS):
                flux[i, h] = stepped(base[i - 1, h], whole_in[h], 0.5 * penalty_ref[:, h, :])
            send_edges(i)
        take(all_terms.at[i, 0 : n_region - 1, 0:SLOTS], recv_sem.at[i, 2])

        received = all_terms[i].reshape(n_region * SPREAD, CELLS)
        sums[i] = (
            dot(pick_t[...], received, ((1,), (0,)))
            .astype(jnp.bfloat16)
            .reshape(LAG * n_region, ROWS, CELLS)
        )
        if i < ITERS - 1:
            at, later_at, earlier_at = 0, {}, {}
            for d in range(1, LAG):
                size = (LAG - d) * n_region
                later_at[d], earlier_at[d] = at, at + size
                at += 2 * size
                for src, start, tm in [(0, later_at[d], later[d]), (d * n_region, earlier_at[d], earlier[d])]:
                    send(
                        sums.at[i, src : src + size], nearby.at[start : start + size],
                        side_sem.at[2, 0], side_sem.at[2, 1], tm, r,
                    )
            take(fields.at[0 : len(others)], side_sem.at[0, 1])
            take(nearby, side_sem.at[2, 1])
            for l in range(LAG):
                rows_of = [(nearby, later_at[d] + (l - d) * n_region) for d in range(1, l + 1)]
                rows_of += [(nearby, earlier_at[d] + l * n_region) for d in range(1, LAG - l)]
                for g in range(n_region):
                    adjoint = sums[i, l * n_region + g].astype(jnp.float32)
                    for ref, start in rows_of:
                        adjoint = adjoint + ref[start + g].astype(jnp.float32)
                    if l == 0:
                        whole_out[g] = adjoint
                    field = fields[l * n_region + g].astype(jnp.float32)
                    window[i + 1, l * n_region + g] = stepped(field[0], adjoint, field[1]).astype(
                        jnp.bfloat16
                    )
        else:
            for l, k in others:
                send(
                    sums.at[i, l * n_region + region[k]], parts.at[l * n_region + r],
                    send_sem.at[i, 3], recv_sem.at[i, 3], earlier[l], region[k],
                )
            parts[r] = sums[i, r]
            make_base(i)
            take(parts.at[0 : len(others)], recv_sem.at[i, 3])
            for h in range(HOURS):
                adjoint = parts[h].astype(jnp.float32)
                for l in range(1, LAG):
                    adjoint = adjoint + parts[l * n_region + h].astype(jnp.float32)
                out_ref[:, h, :] = stepped(base[i, h], adjoint, 0.5 * penalty_ref[:, h, :])

    take(picks.at[0 : n_region - 1], pick_sem.at[0])
    take(window.at[0, 0 : len(others)], send_sem.at[0, 0])
    take(fields.at[0 : len(others)], side_sem.at[0, 0])
    take(whole_in.at[0 : n_region - 1], side_sem.at[1, 0])
    take(nearby, side_sem.at[2, 0])
    take(parts.at[0 : len(others)], send_sem.at[ITERS - 1, 3])
    for i in range(ITERS):
        take(slots.at[i, 0 : n_region - 1], send_sem.at[i, 1])
        take(terms.at[i, 0 : n_region - 1], send_sem.at[i, 2])
        for e in range(2):
            take(edge_rows.at[i, e], edge_send.at[i, e])
            take(edge_hours.at[i, e], edge_send.at[i, 2 + e])


def local(flux_init, penalty, observed, footprint, tile_index):
    n_tm, n_region = lax.axis_size("tm"), lax.axis_size("region")
    tiles = tile_index.shape[0]
    in_vmem = pl.BlockSpec(memory_space=pltpu.VMEM)
    table = LAG * n_region
    half, full = jnp.bfloat16, jnp.float32
    dma = pltpu.SemaphoreType.DMA
    return pl.pallas_call(
        functools.partial(kernel, n_tm, n_region, tiles),
        out_shape=jax.ShapeDtypeStruct(flux_init.shape, full),
        in_specs=[pl.BlockSpec(memory_space=pltpu.HBM)] * 5,
        out_specs=in_vmem,
        scratch_shapes=[
            pltpu.VMEM(flux_init.shape, full),
            pltpu.VMEM(flux_init.shape, full),
            pltpu.VMEM((NOB, OBS), full),
            pltpu.VMEM((4, tiles), jnp.int32),
            pltpu.VMEM((tiles * OBS, HOURS * CELLS), half),
            pltpu.VMEM((HOURS * CELLS, tiles * OBS), half),
            pltpu.VMEM((ITERS, HOURS, ROWS, CELLS), full),
            pltpu.VMEM((HOURS, ROWS, CELLS), half),
            pltpu.VMEM((ITERS, table, ROWS, CELLS), half),
            pltpu.VMEM((ITERS, n_region, SLOTS, CELLS), half),
            pltpu.VMEM((ITERS, n_region, SLOTS, CELLS), half),
            pltpu.VMEM((ITERS, n_region, SLOTS, CELLS), half),
            pltpu.VMEM((ITERS, n_region, SPREAD, CELLS), half),
            pltpu.VMEM((ITERS, table, ROWS, CELLS), half),
            pltpu.VMEM((table, ROWS, CELLS), half),
            pltpu.VMEM((ITERS, HOURS, ROWS, CELLS), full),
            pltpu.VMEM((HOURS, 2, ROWS, CELLS), half),
            pltpu.VMEM((table, 2, ROWS, CELLS), half),
            pltpu.VMEM((LAG * (LAG - 1) * n_region, ROWS, CELLS), half),
            pltpu.VMEM((n_region, ROWS, CELLS), full),
            pltpu.VMEM((n_region, ROWS, CELLS), full),
            pltpu.VMEM((ITERS, 2, HOURS, CELLS), full),
            pltpu.VMEM((ITERS, 2, HOURS, CELLS), full),
            pltpu.VMEM((ITERS, 2, ROWS, CELLS), full),
            pltpu.VMEM((128, 128), jnp.int32),
            pltpu.VMEM((n_region, 8, 128), jnp.int32),
            pltpu.VMEM((n_region * SLOTS, table * ROWS), half),
            pltpu.VMEM((table * ROWS, n_region * SPREAD), half),
            dma,
            dma((4,)),
            dma((2,)),
            dma((ITERS, 4)),
            dma((ITERS, 4)),
            dma((ITERS, n_region)),
            dma((3, 2)),
            dma((ITERS, 4)),
            dma((ITERS, 4)),
        ],
        compiler_params=pltpu.CompilerParams(
            collective_id=0, has_side_effects=True, vmem_limit_bytes=55 * 2**20
        ),
        cost_estimate=pl.CostEstimate(
            flops=8 * footprint.size, bytes_accessed=2 * footprint.size, transcendentals=0
        ),
    )(
        flux_init,
        penalty,
        observed.reshape(NOB, OBS),
        tile_index.T,
        footprint.reshape(tiles * OBS, HOURS * CELLS),
    )


def solution(mesh):
    in_specs = (
        P("region", "tm", None),
        P("region", "tm", None),
        P(("tm", "region")),
        P(("tm", "region"), None, None),
        P(("tm", "region"), None),
    )
    out_specs = P("region", "tm", None)
    return jax.shard_map(local, mesh=mesh, in_specs=in_specs, out_specs=out_specs, check_vma=False)
```

```python
import functools

import jax
import jax.numpy as jnp
from jax import lax
from jax.experimental import pallas as pl
from jax.experimental.pallas import tpu as pltpu
from jax.sharding import PartitionSpec as P

LAG = 4
ITERS = 2
SLOTS = 48
SPREAD = 64
ROWS = 16
HOURS = 8
CELLS = 128
OBS = 128
NOB = 8
GROUP = 16
MESH = pl.DeviceIdType.MESH
HIGHEST = lax.Precision.HIGHEST


def take(ref, sem):
    pltpu.make_async_copy(ref, ref, sem).wait()


def dot(a, b, dims, precision=None):
    return lax.dot_general(
        a, b, (dims, ((), ())), precision=precision, preferred_element_type=jnp.float32
    )


def kernel(
    n_tm,
    n_region,
    tiles,
    flux_hbm,
    penalty_hbm,
    observed_hbm,
    index_hbm,
    footprint_ref,
    out_ref,
    flux_ref,
    penalty_ref,
    observed_ref,
    index_ref,
    foot,
    foot_t,
    flux,
    low,
    window,
    blocks,
    slots,
    terms,
    all_terms,
    sums,
    parts,
    base,
    owned,
    fields,
    nearby,
    whole_out,
    whole_in,
    edges,
    edge_rows,
    edge_hours,
    index_pad,
    picks,
    pick,
    pick_t,
    foot_sem,
    input_sem,
    pick_sem,
    send_sem,
    recv_sem,
    slot_recv,
    side_sem,
    edge_send,
    edge_recv,
):
    w = lax.axis_index("tm")
    r = lax.axis_index("region")
    later = [lax.rem(w + l, n_tm) for l in range(LAG)]
    earlier = [lax.rem(w + n_tm - l, n_tm) for l in range(LAG)]
    region = [lax.rem(r + k, n_region) for k in range(n_region)]
    others = [(l, k) for l in reversed(range(LAG)) for k in range(n_region) if (l, k) != (0, 0)]
    table_rows = LAG * n_region * ROWS
    own = r // 2
    flip = own + 1 - 2 * lax.rem(own, 2)
    pairs = [own, flip, lax.rem(own + 2, 4), lax.rem(flip + 2, 4)]
    partner = r + 1 - 2 * lax.rem(r, 2)
    near_first = [partner] + [2 * q + e for q in pairs[1:] for e in range(2)]

    barrier = pltpu.get_barrier_semaphore()
    for l, k in others:
        pl.semaphore_signal(
            barrier, inc=1, device_id={"tm": earlier[l], "region": region[k]}, device_id_type=MESH
        )
    pl.semaphore_signal(barrier, inc=1, device_id={"tm": later[1], "region": r}, device_id_type=MESH)

    inputs = [
        pltpu.make_async_copy(src, dst, input_sem.at[k])
        for k, (src, dst) in enumerate(
            [
                (flux_hbm, flux_ref),
                (index_hbm, index_ref),
                (observed_hbm, observed_ref),
                (penalty_hbm, penalty_ref),
            ]
        )
    ]
    load = pltpu.make_async_copy(footprint_ref, foot, foot_sem)
    for copy in inputs + [load]:
        copy.start()

    def send(src, dst, sent, received, tm, reg):
        pltpu.make_async_remote_copy(
            src_ref=src,
            dst_ref=dst,
            send_sem=sent,
            recv_sem=received,
            device_id={"tm": tm, "region": reg},
            device_id_type=MESH,
        ).start()

    index_pad[...] = jnp.zeros_like(index_pad)
    all_terms[...] = jnp.zeros_like(all_terms)
    for copy in inputs:
        copy.wait()
    index_pad[0:4, 0:tiles] = index_ref[...]
    entries = index_pad[...]
    lag = entries[1:2, :]
    usable = (entries[3:4, :] == 1) & (lag <= w)
    mine = jnp.where(usable, lag * (n_region * ROWS) + entries[2:3, :], -1)
    picks[r] = jnp.broadcast_to(mine, (8, 128))
    for h in range(HOURS):
        flux[0, h] = flux_ref[:, h, :]
        low[h] = flux[0, h].astype(jnp.bfloat16)

    pl.semaphore_wait(barrier, len(others) + 1)

    def send_edges(i):
        edges[i, 0] = flux[i, :, 0, :]
        edges[i, 1] = flux[i, :, ROWS - 1, :]
        for e, (src, dst, tm, reg) in enumerate(
            [
                (edges.at[i, 1], edge_rows.at[i, 0], w, region[1]),
                (edges.at[i, 0], edge_rows.at[i, 1], w, region[n_region - 1]),
                (flux.at[i, HOURS - 1], edge_hours.at[i, 0], later[1], r),
                (flux.at[i, 0], edge_hours.at[i, 1], earlier[1], r),
            ]
        ):
            send(src, dst, edge_send.at[i, e], edge_recv.at[i, e], tm, reg)

    def make_base(i):
        for e in range(2):
            take(edge_rows.at[i, e], edge_recv.at[i, e])
            take(edge_hours.at[i, e], edge_recv.at[i, 2 + e])
        row_low = jnp.where(r > 0, edge_rows[i, 0], 0.0)
        row_high = jnp.where(r < n_region - 1, edge_rows[i, 1], 0.0)
        hour_low = jnp.where(w > 0, edge_hours[i, 0], 0.0)
        hour_high = jnp.where(w < n_tm - 1, edge_hours[i, 1], 0.0)
        cell = lax.broadcasted_iota(jnp.int32, (ROWS, CELLS), 1)
        planes = [hour_low] + [flux[i, h] for h in range(HOURS)] + [hour_high]
        for h in range(HOURS):
            here = planes[h + 1]
            neighbours = jnp.concatenate([here[1:], row_high[h : h + 1]], axis=0)
            neighbours = neighbours + jnp.concatenate([row_low[h : h + 1], here[:-1]], axis=0)
            neighbours = neighbours + planes[h + 2] + planes[h]
            neighbours = neighbours + jnp.where(cell < CELLS - 1, pltpu.roll(here, CELLS - 1, 1), 0.0)
            neighbours = neighbours + jnp.where(cell > 0, pltpu.roll(here, 1, 1), 0.0)
            base[i, h] = here - 0.1 * (6.0 * here - neighbours)

    def stepped(start, adjoint, cutoff):
        value = start - 0.5 * adjoint
        return value - jnp.clip(value, -cutoff, cutoff)

    for i in range(ITERS):
        if i == 0:
            for l, k in others:
                send(
                    low.at[region[k]], window.at[0, l * n_region + r],
                    send_sem.at[0, 0], recv_sem.at[0, 0], later[l], region[k],
                )
            window[0, r] = low[r]
            for k in range(1, n_region):
                send(picks.at[r], picks.at[r], pick_sem.at[0], pick_sem.at[1], w, region[k])
            send_edges(0)
        if i == 0:
            load.wait()
            for t in range(24):
                foot_t[:, t * OBS : (t + 1) * OBS] = jnp.transpose(foot[t * OBS : (t + 1) * OBS, :])
            for h in range(HOURS):
                owned[h, 1] = (0.5 * penalty_ref[:, h, :]).astype(jnp.bfloat16)
            for l, k in others:
                send(
                    owned.at[region[k], 1], fields.at[l * n_region + r, 1],
                    side_sem.at[0, 0], side_sem.at[0, 1], later[l], region[k],
                )
            fields[r, 1] = owned[r, 1]
            take(picks.at[0 : n_region - 1], pick_sem.at[1])
            rows = picks[:, 0, :]
            columns = jnp.transpose(jnp.concatenate([rows] * 16, axis=0))
            across = lax.broadcasted_iota(jnp.int32, (SLOTS, table_rows), 1)
            for d in range(n_region):
                chosen = columns[0:SLOTS, d : d + 1] == across
                pick[d * SLOTS : (d + 1) * SLOTS, :] = chosen.astype(jnp.float32).astype(jnp.bfloat16)
            lane = lax.broadcasted_iota(jnp.int32, (1, 128), 1)
            moved = pltpu.roll(rows, SPREAD, 1)
            down = lax.broadcasted_iota(jnp.int32, (table_rows, 128), 0)
            for d in range(0, n_region, 2):
                pair = jnp.where(lane < SPREAD, rows[d : d + 1], moved[d + 1 : d + 2])
                chosen = down == pair
                pick_t[:, d * SPREAD : (d + 2) * SPREAD] = chosen.astype(jnp.float32).astype(
                    jnp.bfloat16
                )
            make_base(0)
            for h in range(HOURS):
                owned[h, 0] = base[0, h].astype(jnp.bfloat16)
            take(window.at[0, 0 : len(others)], recv_sem.at[0, 0])

        table = window[i].reshape(table_rows, CELLS)
        for q in reversed(pairs):
            rows_of = pl.ds(pl.multiple_of(q * 2 * SLOTS, 2 * SLOTS), 2 * SLOTS)
            both = dot(pick[rows_of, :], table, ((1,), (0,))).astype(jnp.bfloat16)
            blocks[i, 2 * q] = both[:SLOTS]
            blocks[i, 2 * q + 1] = both[SLOTS:]
            for reg in [2 * q + 1, 2 * q] if q is not own else [partner]:
                send(
                    blocks.at[i, reg], slots.at[i, r],
                    send_sem.at[i, 1], slot_recv.at[i, r], w, reg,
                )
        slots[i, r] = blocks[i, r]
        if i == 0:
            for l, k in others:
                send(
                    owned.at[region[k], 0], fields.at[l * n_region + r, 0],
                    side_sem.at[0, 0], side_sem.at[0, 1], later[l], region[k],
                )
            fields[r, 0] = owned[r, 0]
            for t in range(24, tiles):
                foot_t[:, t * OBS : (t + 1) * OBS] = jnp.transpose(foot[t * OBS : (t + 1) * OBS, :])
        else:
            for reg in reversed(near_first):
                send(whole_out.at[reg], whole_in.at[r], side_sem.at[1, 0], side_sem.at[1, 1], w, reg)
            whole_in[r] = whole_out[r]

        down = lax.broadcasted_iota(jnp.int32, (GROUP, OBS), 0)
        groups = [(first, min(first + GROUP, tiles)) for first in range(0, SLOTS, GROUP)]
        products = [jnp.zeros((GROUP, OBS), jnp.float32) for _ in groups]
        for step, q in enumerate(pairs):
            for reg in [2 * q, 2 * q + 1] if step else [partner]:
                take(slots.at[i, reg], slot_recv.at[i, reg])
            x = jnp.concatenate([slots[i, 2 * q], slots[i, 2 * q + 1]], axis=1)
            cells = pl.ds(pl.multiple_of(q * 2 * CELLS, 2 * CELLS), 2 * CELLS)
            for g, (first, last) in enumerate(groups):
                x_group = x[first : first + GROUP, :]
                total = jnp.zeros((GROUP, OBS), jnp.float32)
                for t in range(first, last, 2):
                    both = dot(x_group, foot_t[cells, t * OBS : (t + 2) * OBS], ((1,), (0,)))
                    total = jnp.where(down == t - first, both[:, :OBS], total)
                    total = jnp.where(down == t + 1 - first, both[:, OBS:], total)
                products[g] = products[g] + total
        products = jnp.concatenate(products, axis=0)
        row_block = index_pad[0:1, 0:SLOTS]
        selector = (lax.broadcasted_iota(jnp.int32, (NOB, SLOTS), 0) == row_block).astype(jnp.float32)
        predicted = dot(selector, products, ((1,), (0,)), HIGHEST)
        residual = (predicted - observed_ref[...]).astype(jnp.bfloat16).astype(jnp.float32)

        spread = jnp.zeros((SLOTS, OBS), jnp.float32)
        block_of = jnp.transpose(index_pad[...])[0:SLOTS, 0:1]
        for b in range(NOB):
            spread = jnp.where(block_of == b, residual[b : b + 1, :], spread)
        lefts = []
        for first in range(0, SLOTS, GROUP):
            part = spread[first : first + GROUP, :]
            lefts.append(
                jnp.concatenate(
                    [
                        jnp.where(down == t - first, part, 0.0)
                        for t in range(first, min(first + GROUP, tiles))
                    ],
                    axis=1,
                ).astype(jnp.bfloat16)
            )
        for q in reversed(pairs):
            cells = pl.ds(pl.multiple_of(q * 2 * CELLS, 2 * CELLS), 2 * CELLS)
            for g, (first, last) in enumerate(groups):
                both = dot(
                    lefts[g], foot[first * OBS : last * OBS, cells], ((1,), (0,))
                ).astype(jnp.bfloat16)
                terms[i, 2 * q, first : first + GROUP, :] = both[:, :CELLS]
                terms[i, 2 * q + 1, first : first + GROUP, :] = both[:, CELLS:]
            for reg in [2 * q, 2 * q + 1] if q is not own else [partner]:
                send(
                    terms.at[i, reg], all_terms.at[i, r, 0:SLOTS],
                    send_sem.at[i, 2], recv_sem.at[i, 2], w, reg,
                )
        all_terms[i, r, 0:SLOTS] = terms[i, r]
        if i > 0:
            take(whole_in.at[0 : n_region - 1], side_sem.at[1, 1])
            for h in range(HOURS):
                flux[i, h] = stepped(base[i - 1, h], whole_in[h], 0.5 * penalty_ref[:, h, :])
            send_edges(i)
        take(all_terms.at[i, 0 : n_region - 1, 0:SLOTS], recv_sem.at[i, 2])

        received = all_terms[i].reshape(n_region * SPREAD, CELLS)
        lag_rows = n_region * ROWS
        at, later_at, earlier_at = 0, {}, {}
        for d in range(1, LAG):
            size = (LAG - d) * n_region
            later_at[d], earlier_at[d] = at, at + size
            at += 2 * size
        ready = set()
        waiting = [(d, side) for d in reversed(range(1, LAG)) for side in (0, 1)]
        for l in [3, 0, 1, 2] if i < ITERS - 1 else [3, 2, 1, 0]:
            part = dot(pick_t[l * lag_rows : (l + 1) * lag_rows, :], received, ((1,), (0,)))
            sums[i, l * n_region : (l + 1) * n_region] = part.astype(jnp.bfloat16).reshape(
                n_region, ROWS, CELLS
            )
            ready.add(l)
            for d, side in list(waiting) if i < ITERS - 1 else []:
                first = d * side
                if not ready.issuperset(range(first, first + LAG - d)):
                    continue
                waiting.remove((d, side))
                size = (LAG - d) * n_region
                start = earlier_at[d] if side else later_at[d]
                send(
                    sums.at[i, first * n_region : first * n_region + size],
                    nearby.at[start : start + size],
                    side_sem.at[2, 0], side_sem.at[2, 1], earlier[d] if side else later[d], r,
                )
            if i == ITERS - 1:
                for k in reversed(range(1 if l == 0 else 0, n_region)):
                    send(
                        sums.at[i, l * n_region + region[k]], parts.at[l * n_region + r],
                        send_sem.at[i, 3], recv_sem.at[i, 3], earlier[l], region[k],
                    )
        if i < ITERS - 1:
            take(fields.at[0 : len(others)], side_sem.at[0, 1])
            take(nearby, side_sem.at[2, 1])
            for l in range(LAG):
                rows_of = [(nearby, later_at[d] + (l - d) * n_region) for d in range(1, l + 1)]
                rows_of += [(nearby, earlier_at[d] + l * n_region) for d in range(1, LAG - l)]
                for g in range(n_region):
                    adjoint = sums[i, l * n_region + g].astype(jnp.float32)
                    for ref, start in rows_of:
                        adjoint = adjoint + ref[start + g].astype(jnp.float32)
                    if l == 0:
                        whole_out[g] = adjoint
                    field = fields[l * n_region + g].astype(jnp.float32)
                    window[i + 1, l * n_region + g] = stepped(field[0], adjoint, field[1]).astype(
                        jnp.bfloat16
                    )
        else:
            parts[r] = sums[i, r]
            make_base(i)
            take(parts.at[0 : len(others)], recv_sem.at[i, 3])
            for h in range(HOURS):
                adjoint = parts[h].astype(jnp.float32)
                for l in range(1, LAG):
                    adjoint = adjoint + parts[l * n_region + h].astype(jnp.float32)
                out_ref[:, h, :] = stepped(base[i, h], adjoint, 0.5 * penalty_ref[:, h, :])

    take(picks.at[0 : n_region - 1], pick_sem.at[0])
    take(window.at[0, 0 : len(others)], send_sem.at[0, 0])
    take(fields.at[0 : len(others)], side_sem.at[0, 0])
    take(whole_in.at[0 : n_region - 1], side_sem.at[1, 0])
    take(nearby, side_sem.at[2, 0])
    take(parts.at[0 : len(others)], send_sem.at[ITERS - 1, 3])
    for i in range(ITERS):
        take(slots.at[i, 0 : n_region - 1], send_sem.at[i, 1])
        take(terms.at[i, 0 : n_region - 1], send_sem.at[i, 2])
        for e in range(2):
            take(edge_rows.at[i, e], edge_send.at[i, e])
            take(edge_hours.at[i, e], edge_send.at[i, 2 + e])


def local(flux_init, penalty, observed, footprint, tile_index):
    n_tm, n_region = lax.axis_size("tm"), lax.axis_size("region")
    tiles = tile_index.shape[0]
    in_vmem = pl.BlockSpec(memory_space=pltpu.VMEM)
    table = LAG * n_region
    half, full = jnp.bfloat16, jnp.float32
    dma = pltpu.SemaphoreType.DMA
    return pl.pallas_call(
        functools.partial(kernel, n_tm, n_region, tiles),
        out_shape=jax.ShapeDtypeStruct(flux_init.shape, full),
        in_specs=[pl.BlockSpec(memory_space=pltpu.HBM)] * 5,
        out_specs=in_vmem,
        scratch_shapes=[
            pltpu.VMEM(flux_init.shape, full),
            pltpu.VMEM(flux_init.shape, full),
            pltpu.VMEM((NOB, OBS), full),
            pltpu.VMEM((4, tiles), jnp.int32),
            pltpu.VMEM((tiles * OBS, HOURS * CELLS), half),
            pltpu.VMEM((HOURS * CELLS, tiles * OBS), half),
            pltpu.VMEM((ITERS, HOURS, ROWS, CELLS), full),
            pltpu.VMEM((HOURS, ROWS, CELLS), half),
            pltpu.VMEM((ITERS, table, ROWS, CELLS), half),
            pltpu.VMEM((ITERS, n_region, SLOTS, CELLS), half),
            pltpu.VMEM((ITERS, n_region, SLOTS, CELLS), half),
            pltpu.VMEM((ITERS, n_region, SLOTS, CELLS), half),
            pltpu.VMEM((ITERS, n_region, SPREAD, CELLS), half),
            pltpu.VMEM((ITERS, table, ROWS, CELLS), half),
            pltpu.VMEM((table, ROWS, CELLS), half),
            pltpu.VMEM((ITERS, HOURS, ROWS, CELLS), full),
            pltpu.VMEM((HOURS, 2, ROWS, CELLS), half),
            pltpu.VMEM((table, 2, ROWS, CELLS), half),
            pltpu.VMEM((LAG * (LAG - 1) * n_region, ROWS, CELLS), half),
            pltpu.VMEM((n_region, ROWS, CELLS), full),
            pltpu.VMEM((n_region, ROWS, CELLS), full),
            pltpu.VMEM((ITERS, 2, HOURS, CELLS), full),
            pltpu.VMEM((ITERS, 2, HOURS, CELLS), full),
            pltpu.VMEM((ITERS, 2, ROWS, CELLS), full),
            pltpu.VMEM((128, 128), jnp.int32),
            pltpu.VMEM((n_region, 8, 128), jnp.int32),
            pltpu.VMEM((n_region * SLOTS, table * ROWS), half),
            pltpu.VMEM((table * ROWS, n_region * SPREAD), half),
            dma,
            dma((4,)),
            dma((2,)),
            dma((ITERS, 4)),
            dma((ITERS, 4)),
            dma((ITERS, n_region)),
            dma((3, 2)),
            dma((ITERS, 4)),
            dma((ITERS, 4)),
        ],
        compiler_params=pltpu.CompilerParams(
            collective_id=0, has_side_effects=True, vmem_limit_bytes=55 * 2**20
        ),
        cost_estimate=pl.CostEstimate(
            flops=8 * footprint.size, bytes_accessed=2 * footprint.size, transcendentals=0
        ),
    )(
        flux_init,
        penalty,
        observed.reshape(NOB, OBS),
        tile_index.T,
        footprint.reshape(tiles * OBS, HOURS * CELLS),
    )


def solution(mesh):
    in_specs = (
        P("region", "tm", None),
        P("region", "tm", None),
        P(("tm", "region")),
        P(("tm", "region"), None, None),
        P(("tm", "region"), None),
    )
    out_specs = P("region", "tm", None)
    return jax.shard_map(local, mesh=mesh, in_specs=in_specs, out_specs=out_specs, check_vma=False)
```

```python
import functools

import jax
import jax.numpy as jnp
from jax import lax
from jax.experimental import pallas as pl
from jax.experimental.pallas import tpu as pltpu
from jax.sharding import PartitionSpec as P

LAG = 4
ITERS = 2
SLOTS = 48
SPREAD = 64
ROWS = 16
HOURS = 8
CELLS = 128
OBS = 128
NOB = 8
GROUP = 16
MESH = pl.DeviceIdType.MESH
HIGHEST = lax.Precision.HIGHEST


def take(ref, sem):
    pltpu.make_async_copy(ref, ref, sem).wait()


def dot(a, b, dims, precision=None):
    return lax.dot_general(
        a, b, (dims, ((), ())), precision=precision, preferred_element_type=jnp.float32
    )


def kernel(
    n_tm,
    n_region,
    tiles,
    flux_hbm,
    penalty_hbm,
    observed_hbm,
    index_hbm,
    footprint_ref,
    out_ref,
    flux_ref,
    penalty_ref,
    observed_ref,
    index_ref,
    foot,
    foot_t,
    flux,
    low,
    window,
    blocks,
    slots,
    terms,
    all_terms,
    sums,
    parts,
    base,
    owned,
    fields,
    nearby,
    whole_out,
    whole_in,
    edges,
    edge_rows,
    edge_hours,
    index_pad,
    picks,
    pick,
    pick_t,
    foot_sem,
    input_sem,
    pick_sem,
    send_sem,
    recv_sem,
    slot_recv,
    side_sem,
    edge_send,
    edge_recv,
):
    w = lax.axis_index("tm")
    r = lax.axis_index("region")
    later = [lax.rem(w + l, n_tm) for l in range(LAG)]
    earlier = [lax.rem(w + n_tm - l, n_tm) for l in range(LAG)]
    region = [lax.rem(r + k, n_region) for k in range(n_region)]
    others = [(l, k) for l in reversed(range(LAG)) for k in range(n_region) if (l, k) != (0, 0)]
    table_rows = LAG * n_region * ROWS
    own = r // 2
    flip = own + 1 - 2 * lax.rem(own, 2)
    pairs = [own, flip, lax.rem(own + 2, 4), lax.rem(flip + 2, 4)]
    partner = r + 1 - 2 * lax.rem(r, 2)
    near_first = [partner] + [2 * q + e for q in pairs[1:] for e in range(2)]

    barrier = pltpu.get_barrier_semaphore()
    for l, k in others:
        pl.semaphore_signal(
            barrier, inc=1, device_id={"tm": earlier[l], "region": region[k]}, device_id_type=MESH
        )
    pl.semaphore_signal(barrier, inc=1, device_id={"tm": later[1], "region": r}, device_id_type=MESH)

    inputs = [
        pltpu.make_async_copy(src, dst, input_sem.at[k])
        for k, (src, dst) in enumerate(
            [
                (flux_hbm, flux_ref),
                (index_hbm, index_ref),
                (observed_hbm, observed_ref),
                (penalty_hbm, penalty_ref),
            ]
        )
    ]
    load = pltpu.make_async_copy(footprint_ref, foot, foot_sem)
    for copy in inputs + [load]:
        copy.start()

    def send(src, dst, sent, received, tm, reg):
        pltpu.make_async_remote_copy(
            src_ref=src,
            dst_ref=dst,
            send_sem=sent,
            recv_sem=received,
            device_id={"tm": tm, "region": reg},
            device_id_type=MESH,
        ).start()

    index_pad[...] = jnp.zeros_like(index_pad)
    all_terms[...] = jnp.zeros_like(all_terms)
    for copy in inputs:
        copy.wait()
    index_pad[0:4, 0:tiles] = index_ref[...]
    entries = index_pad[...]
    lag = entries[1:2, :]
    usable = (entries[3:4, :] == 1) & (lag <= w)
    mine = jnp.where(usable, lag * (n_region * ROWS) + entries[2:3, :], -1)
    picks[r] = jnp.broadcast_to(mine, (8, 128))
    for h in range(HOURS):
        flux[0, h] = flux_ref[:, h, :]
        low[h] = flux[0, h].astype(jnp.bfloat16)

    pl.semaphore_wait(barrier, len(others) + 1)

    def send_edges(i):
        edges[i, 0] = flux[i, :, 0, :]
        edges[i, 1] = flux[i, :, ROWS - 1, :]
        for e, (src, dst, tm, reg) in enumerate(
            [
                (edges.at[i, 1], edge_rows.at[i, 0], w, region[1]),
                (edges.at[i, 0], edge_rows.at[i, 1], w, region[n_region - 1]),
                (flux.at[i, HOURS - 1], edge_hours.at[i, 0], later[1], r),
                (flux.at[i, 0], edge_hours.at[i, 1], earlier[1], r),
            ]
        ):
            send(src, dst, edge_send.at[i, e], edge_recv.at[i, e], tm, reg)

    def make_base(i):
        for e in range(2):
            take(edge_rows.at[i, e], edge_recv.at[i, e])
            take(edge_hours.at[i, e], edge_recv.at[i, 2 + e])
        row_low = jnp.where(r > 0, edge_rows[i, 0], 0.0)
        row_high = jnp.where(r < n_region - 1, edge_rows[i, 1], 0.0)
        hour_low = jnp.where(w > 0, edge_hours[i, 0], 0.0)
        hour_high = jnp.where(w < n_tm - 1, edge_hours[i, 1], 0.0)
        cell = lax.broadcasted_iota(jnp.int32, (ROWS, CELLS), 1)
        planes = [hour_low] + [flux[i, h] for h in range(HOURS)] + [hour_high]
        for h in range(HOURS):
            here = planes[h + 1]
            neighbours = jnp.concatenate([here[1:], row_high[h : h + 1]], axis=0)
            neighbours = neighbours + jnp.concatenate([row_low[h : h + 1], here[:-1]], axis=0)
            neighbours = neighbours + planes[h + 2] + planes[h]
            neighbours = neighbours + jnp.where(cell < CELLS - 1, pltpu.roll(here, CELLS - 1, 1), 0.0)
            neighbours = neighbours + jnp.where(cell > 0, pltpu.roll(here, 1, 1), 0.0)
            base[i, h] = here - 0.1 * (6.0 * here - neighbours)

    def stepped(start, adjoint, cutoff):
        value = start - 0.5 * adjoint
        return value - jnp.clip(value, -cutoff, cutoff)

    for i in range(ITERS):
        if i == 0:
            for l in reversed(range(LAG)):
                for reg in near_first[::-1] + ([r] if l else []):
                    send(
                        low.at[reg], window.at[0, l * n_region + r],
                        send_sem.at[0, 0], recv_sem.at[0, 0], later[l], reg,
                    )
            window[0, r] = low[r]
            for k in range(1, n_region):
                send(picks.at[r], picks.at[r], pick_sem.at[0], pick_sem.at[1], w, region[k])
            send_edges(0)
        if i == 0:
            load.wait()
            for t in range(24):
                foot_t[:, t * OBS : (t + 1) * OBS] = jnp.transpose(foot[t * OBS : (t + 1) * OBS, :])
            for h in range(HOURS):
                owned[h, 1] = (0.5 * penalty_ref[:, h, :]).astype(jnp.bfloat16)
            for l, k in others:
                send(
                    owned.at[region[k], 1], fields.at[l * n_region + r, 1],
                    side_sem.at[0, 0], side_sem.at[0, 1], later[l], region[k],
                )
            fields[r, 1] = owned[r, 1]
            take(picks.at[0 : n_region - 1], pick_sem.at[1])
            rows = picks[:, 0, :]
            columns = jnp.transpose(jnp.concatenate([rows] * 16, axis=0))
            across = lax.broadcasted_iota(jnp.int32, (SLOTS, table_rows), 1)
            for d in range(n_region):
                chosen = columns[0:SLOTS, d : d + 1] == across
                pick[d * SLOTS : (d + 1) * SLOTS, :] = chosen.astype(jnp.float32).astype(jnp.bfloat16)
            lane = lax.broadcasted_iota(jnp.int32, (1, 128), 1)
            moved = pltpu.roll(rows, SPREAD, 1)
            down = lax.broadcasted_iota(jnp.int32, (table_rows, 128), 0)
            for d in range(0, n_region, 2):
                pair = jnp.where(lane < SPREAD, rows[d : d + 1], moved[d + 1 : d + 2])
                chosen = down == pair
                pick_t[:, d * SPREAD : (d + 2) * SPREAD] = chosen.astype(jnp.float32).astype(
                    jnp.bfloat16
                )
            make_base(0)
            for h in range(HOURS):
                owned[h, 0] = base[0, h].astype(jnp.bfloat16)
            take(window.at[0, 0 : len(others)], recv_sem.at[0, 0])

        table = window[i].reshape(table_rows, CELLS)
        for q in reversed(pairs):
            rows_of = pl.ds(pl.multiple_of(q * 2 * SLOTS, 2 * SLOTS), 2 * SLOTS)
            both = dot(pick[rows_of, :], table, ((1,), (0,))).astype(jnp.bfloat16)
            blocks[i, 2 * q] = both[:SLOTS]
            blocks[i, 2 * q + 1] = both[SLOTS:]
            for reg in [2 * q + 1, 2 * q] if q is not own else [partner]:
                send(
                    blocks.at[i, reg], slots.at[i, r],
                    send_sem.at[i, 1], slot_recv.at[i, r], w, reg,
                )
        slots[i, r] = blocks[i, r]
        if i == 0:
            for l, k in others:
                send(
                    owned.at[region[k], 0], fields.at[l * n_region + r, 0],
                    side_sem.at[0, 0], side_sem.at[0, 1], later[l], region[k],
                )
            fields[r, 0] = owned[r, 0]
            for t in range(24, tiles):
                foot_t[:, t * OBS : (t + 1) * OBS] = jnp.transpose(foot[t * OBS : (t + 1) * OBS, :])
        else:
            for reg in reversed(near_first):
                send(whole_out.at[reg], whole_in.at[r], side_sem.at[1, 0], side_sem.at[1, 1], w, reg)
            whole_in[r] = whole_out[r]

        down = lax.broadcasted_iota(jnp.int32, (GROUP, OBS), 0)
        groups = [(first, min(first + GROUP, tiles)) for first in range(0, SLOTS, GROUP)]
        products = [jnp.zeros((GROUP, OBS), jnp.float32) for _ in groups]
        for step, q in enumerate(pairs):
            for reg in [2 * q, 2 * q + 1] if step else [partner]:
                take(slots.at[i, reg], slot_recv.at[i, reg])
            x = jnp.concatenate([slots[i, 2 * q], slots[i, 2 * q + 1]], axis=1)
            cells = pl.ds(pl.multiple_of(q * 2 * CELLS, 2 * CELLS), 2 * CELLS)
            for g, (first, last) in enumerate(groups):
                x_group = x[first : first + GROUP, :]
                total = jnp.zeros((GROUP, OBS), jnp.float32)
                for t in range(first, last, 2):
                    both = dot(x_group, foot_t[cells, t * OBS : (t + 2) * OBS], ((1,), (0,)))
                    total = jnp.where(down == t - first, both[:, :OBS], total)
                    total = jnp.where(down == t + 1 - first, both[:, OBS:], total)
                products[g] = products[g] + total
        products = jnp.concatenate(products, axis=0)
        row_block = index_pad[0:1, 0:SLOTS]
        selector = (lax.broadcasted_iota(jnp.int32, (NOB, SLOTS), 0) == row_block).astype(jnp.float32)
        predicted = dot(selector, products, ((1,), (0,)), HIGHEST)
        residual = (predicted - observed_ref[...]).astype(jnp.bfloat16).astype(jnp.float32)

        spread = jnp.zeros((SLOTS, OBS), jnp.float32)
        block_of = jnp.transpose(index_pad[...])[0:SLOTS, 0:1]
        for b in range(NOB):
            spread = jnp.where(block_of == b, residual[b : b + 1, :], spread)
        lefts = []
        for first in range(0, SLOTS, GROUP):
            part = spread[first : first + GROUP, :]
            lefts.append(
                jnp.concatenate(
                    [
                        jnp.where(down == t - first, part, 0.0)
                        for t in range(first, min(first + GROUP, tiles))
                    ],
                    axis=1,
                ).astype(jnp.bfloat16)
            )
        for q in reversed(pairs):
            cells = pl.ds(pl.multiple_of(q * 2 * CELLS, 2 * CELLS), 2 * CELLS)
            for g, (first, last) in enumerate(groups):
                both = dot(
                    lefts[g], foot[first * OBS : last * OBS, cells], ((1,), (0,))
                ).astype(jnp.bfloat16)
                terms[i, 2 * q, first : first + GROUP, :] = both[:, :CELLS]
                terms[i, 2 * q + 1, first : first + GROUP, :] = both[:, CELLS:]
            for reg in [2 * q, 2 * q + 1] if q is not own else [partner]:
                send(
                    terms.at[i, reg], all_terms.at[i, r, 0:SLOTS],
                    send_sem.at[i, 2], recv_sem.at[i, 2], w, reg,
                )
        all_terms[i, r, 0:SLOTS] = terms[i, r]
        if i > 0:
            take(whole_in.at[0 : n_region - 1], side_sem.at[1, 1])
            for h in range(HOURS):
                flux[i, h] = stepped(base[i - 1, h], whole_in[h], 0.5 * penalty_ref[:, h, :])
            send_edges(i)
        take(all_terms.at[i, 0 : n_region - 1, 0:SLOTS], recv_sem.at[i, 2])

        received = all_terms[i].reshape(n_region * SPREAD, CELLS)
        lag_rows = n_region * ROWS
        at, later_at, earlier_at = 0, {}, {}
        for d in range(1, LAG):
            size = (LAG - d) * n_region
            later_at[d], earlier_at[d] = at, at + size
            at += 2 * size
        ready = set()
        waiting = [(d, side) for d in reversed(range(1, LAG)) for side in (0, 1)]
        for l in [3, 0, 1, 2] if i < ITERS - 1 else [3, 2, 1, 0]:
            part = dot(pick_t[l * lag_rows : (l + 1) * lag_rows, :], received, ((1,), (0,)))
            sums[i, l * n_region : (l + 1) * n_region] = part.astype(jnp.bfloat16).reshape(
                n_region, ROWS, CELLS
            )
            ready.add(l)
            for d, side in list(waiting) if i < ITERS - 1 else []:
                first = d * side
                if not ready.issuperset(range(first, first + LAG - d)):
                    continue
                waiting.remove((d, side))
                size = (LAG - d) * n_region
                start = earlier_at[d] if side else later_at[d]
                send(
                    sums.at[i, first * n_region : first * n_region + size],
                    nearby.at[start : start + size],
                    side_sem.at[2, 0], side_sem.at[2, 1], earlier[d] if side else later[d], r,
                )
            if i == ITERS - 1:
                for reg in near_first[::-1] + ([r] if l else []):
                    send(
                        sums.at[i, l * n_region + reg], parts.at[l * n_region + r],
                        send_sem.at[i, 3], recv_sem.at[i, 3], earlier[l], reg,
                    )
        if i < ITERS - 1:
            take(fields.at[0 : len(others)], side_sem.at[0, 1])
            take(nearby, side_sem.at[2, 1])
            for l in range(LAG):
                rows_of = [(nearby, later_at[d] + (l - d) * n_region) for d in range(1, l + 1)]
                rows_of += [(nearby, earlier_at[d] + l * n_region) for d in range(1, LAG - l)]
                for g in range(n_region):
                    adjoint = sums[i, l * n_region + g].astype(jnp.float32)
                    for ref, start in rows_of:
                        adjoint = adjoint + ref[start + g].astype(jnp.float32)
                    if l == 0:
                        whole_out[g] = adjoint
                    field = fields[l * n_region + g].astype(jnp.float32)
                    window[i + 1, l * n_region + g] = stepped(field[0], adjoint, field[1]).astype(
                        jnp.bfloat16
                    )
        else:
            parts[r] = sums[i, r]
            make_base(i)
            take(parts.at[0 : len(others)], recv_sem.at[i, 3])
            for h in range(HOURS):
                adjoint = parts[h].astype(jnp.float32)
                for l in range(1, LAG):
                    adjoint = adjoint + parts[l * n_region + h].astype(jnp.float32)
                out_ref[:, h, :] = stepped(base[i, h], adjoint, 0.5 * penalty_ref[:, h, :])

    take(picks.at[0 : n_region - 1], pick_sem.at[0])
    take(window.at[0, 0 : len(others)], send_sem.at[0, 0])
    take(fields.at[0 : len(others)], side_sem.at[0, 0])
    take(whole_in.at[0 : n_region - 1], side_sem.at[1, 0])
    take(nearby, side_sem.at[2, 0])
    take(parts.at[0 : len(others)], send_sem.at[ITERS - 1, 3])
    for i in range(ITERS):
        take(slots.at[i, 0 : n_region - 1], send_sem.at[i, 1])
        take(terms.at[i, 0 : n_region - 1], send_sem.at[i, 2])
        for e in range(2):
            take(edge_rows.at[i, e], edge_send.at[i, e])
            take(edge_hours.at[i, e], edge_send.at[i, 2 + e])


def local(flux_init, penalty, observed, footprint, tile_index):
    n_tm, n_region = lax.axis_size("tm"), lax.axis_size("region")
    tiles = tile_index.shape[0]
    in_vmem = pl.BlockSpec(memory_space=pltpu.VMEM)
    table = LAG * n_region
    half, full = jnp.bfloat16, jnp.float32
    dma = pltpu.SemaphoreType.DMA
    return pl.pallas_call(
        functools.partial(kernel, n_tm, n_region, tiles),
        out_shape=jax.ShapeDtypeStruct(flux_init.shape, full),
        in_specs=[pl.BlockSpec(memory_space=pltpu.HBM)] * 5,
        out_specs=in_vmem,
        scratch_shapes=[
            pltpu.VMEM(flux_init.shape, full),
            pltpu.VMEM(flux_init.shape, full),
            pltpu.VMEM((NOB, OBS), full),
            pltpu.VMEM((4, tiles), jnp.int32),
            pltpu.VMEM((tiles * OBS, HOURS * CELLS), half),
            pltpu.VMEM((HOURS * CELLS, tiles * OBS), half),
            pltpu.VMEM((ITERS, HOURS, ROWS, CELLS), full),
            pltpu.VMEM((HOURS, ROWS, CELLS), half),
            pltpu.VMEM((ITERS, table, ROWS, CELLS), half),
            pltpu.VMEM((ITERS, n_region, SLOTS, CELLS), half),
            pltpu.VMEM((ITERS, n_region, SLOTS, CELLS), half),
            pltpu.VMEM((ITERS, n_region, SLOTS, CELLS), half),
            pltpu.VMEM((ITERS, n_region, SPREAD, CELLS), half),
            pltpu.VMEM((ITERS, table, ROWS, CELLS), half),
            pltpu.VMEM((table, ROWS, CELLS), half),
            pltpu.VMEM((ITERS, HOURS, ROWS, CELLS), full),
            pltpu.VMEM((HOURS, 2, ROWS, CELLS), half),
            pltpu.VMEM((table, 2, ROWS, CELLS), half),
            pltpu.VMEM((LAG * (LAG - 1) * n_region, ROWS, CELLS), half),
            pltpu.VMEM((n_region, ROWS, CELLS), full),
            pltpu.VMEM((n_region, ROWS, CELLS), full),
            pltpu.VMEM((ITERS, 2, HOURS, CELLS), full),
            pltpu.VMEM((ITERS, 2, HOURS, CELLS), full),
            pltpu.VMEM((ITERS, 2, ROWS, CELLS), full),
            pltpu.VMEM((128, 128), jnp.int32),
            pltpu.VMEM((n_region, 8, 128), jnp.int32),
            pltpu.VMEM((n_region * SLOTS, table * ROWS), half),
            pltpu.VMEM((table * ROWS, n_region * SPREAD), half),
            dma,
            dma((4,)),
            dma((2,)),
            dma((ITERS, 4)),
            dma((ITERS, 4)),
            dma((ITERS, n_region)),
            dma((3, 2)),
            dma((ITERS, 4)),
            dma((ITERS, 4)),
        ],
        compiler_params=pltpu.CompilerParams(
            collective_id=0, has_side_effects=True, vmem_limit_bytes=55 * 2**20
        ),
        cost_estimate=pl.CostEstimate(
            flops=8 * footprint.size, bytes_accessed=2 * footprint.size, transcendentals=0
        ),
    )(
        flux_init,
        penalty,
        observed.reshape(NOB, OBS),
        tile_index.T,
        footprint.reshape(tiles * OBS, HOURS * CELLS),
    )


def solution(mesh):
    in_specs = (
        P("region", "tm", None),
        P("region", "tm", None),
        P(("tm", "region")),
        P(("tm", "region"), None, None),
        P(("tm", "region"), None),
    )
    out_specs = P("region", "tm", None)
    return jax.shard_map(local, mesh=mesh, in_specs=in_specs, out_specs=out_specs, check_vma=False)
```

```python
import functools

import jax
import jax.numpy as jnp
from jax import lax
from jax.experimental import pallas as pl
from jax.experimental.pallas import tpu as pltpu
from jax.sharding import PartitionSpec as P

LAG = 4
ITERS = 2
SLOTS = 48
SPREAD = 64
ROWS = 16
HOURS = 8
CELLS = 128
OBS = 128
NOB = 8
GROUP = 16
MESH = pl.DeviceIdType.MESH


def take(ref, sem):
    pltpu.make_async_copy(ref, ref, sem).wait()


def dot(a, b, dims):
    return lax.dot_general(a, b, (dims, ((), ())), preferred_element_type=jnp.float32)


def kernel(
    n_tm,
    n_region,
    tiles,
    flux_hbm,
    penalty_hbm,
    observed_hbm,
    index_hbm,
    footprint_ref,
    out_ref,
    flux_ref,
    penalty_ref,
    observed_ref,
    index_ref,
    foot,
    foot_t,
    flux,
    low,
    window,
    blocks,
    slots,
    terms,
    all_terms,
    sums,
    parts,
    base,
    owned,
    fields,
    nearby,
    whole_out,
    whole_in,
    edges,
    edge_rows,
    edge_hours,
    index_pad,
    block_of,
    picks,
    pick,
    pick_t,
    foot_sem,
    input_sem,
    pick_sem,
    send_sem,
    recv_sem,
    slot_recv,
    side_sem,
    edge_send,
    edge_recv,
):
    w = lax.axis_index("tm")
    r = lax.axis_index("region")
    later = [lax.rem(w + l, n_tm) for l in range(LAG)]
    earlier = [lax.rem(w + n_tm - l, n_tm) for l in range(LAG)]
    region = [lax.rem(r + k, n_region) for k in range(n_region)]
    others = [(l, k) for l in reversed(range(LAG)) for k in range(n_region) if (l, k) != (0, 0)]
    table_rows = LAG * n_region * ROWS
    own = r // 2
    flip = own + 1 - 2 * lax.rem(own, 2)
    pairs = [own, flip, lax.rem(own + 2, 4), lax.rem(flip + 2, 4)]
    partner = r + 1 - 2 * lax.rem(r, 2)
    near_first = [partner] + [2 * q + e for q in pairs[1:] for e in range(2)]

    barrier = pltpu.get_barrier_semaphore()
    for l, k in others:
        pl.semaphore_signal(
            barrier, inc=1, device_id={"tm": earlier[l], "region": region[k]}, device_id_type=MESH
        )
    pl.semaphore_signal(barrier, inc=1, device_id={"tm": later[1], "region": r}, device_id_type=MESH)

    inputs = [
        pltpu.make_async_copy(src, dst, input_sem.at[k])
        for k, (src, dst) in enumerate(
            [
                (flux_hbm, flux_ref),
                (index_hbm, index_ref),
                (observed_hbm, observed_ref),
                (penalty_hbm, penalty_ref),
            ]
        )
    ]
    load = pltpu.make_async_copy(footprint_ref, foot, foot_sem)
    for copy in inputs + [load]:
        copy.start()

    def send(src, dst, sent, received, tm, reg):
        pltpu.make_async_remote_copy(
            src_ref=src,
            dst_ref=dst,
            send_sem=sent,
            recv_sem=received,
            device_id={"tm": tm, "region": reg},
            device_id_type=MESH,
        ).start()

    index_pad[...] = jnp.zeros_like(index_pad)
    all_terms[...] = jnp.zeros_like(all_terms)
    for copy in inputs:
        copy.wait()
    index_pad[0:4, 0:tiles] = index_ref[...]
    entries = index_pad[...]
    lag = entries[1:2, :]
    usable = (entries[3:4, :] == 1) & (lag <= w)
    mine = jnp.where(usable, lag * (n_region * ROWS) + entries[2:3, :], -1)
    picks[r] = jnp.broadcast_to(mine, (8, 128))
    for h in range(HOURS):
        flux[0, h] = flux_ref[:, h, :]
        low[h] = flux[0, h].astype(jnp.bfloat16)

    pl.semaphore_wait(barrier, len(others) + 1)

    def send_edges(i):
        edges[i, 0] = flux[i, :, 0, :]
        edges[i, 1] = flux[i, :, ROWS - 1, :]
        for e, (src, dst, tm, reg) in enumerate(
            [
                (edges.at[i, 1], edge_rows.at[i, 0], w, region[1]),
                (edges.at[i, 0], edge_rows.at[i, 1], w, region[n_region - 1]),
                (flux.at[i, HOURS - 1], edge_hours.at[i, 0], later[1], r),
                (flux.at[i, 0], edge_hours.at[i, 1], earlier[1], r),
            ]
        ):
            send(src, dst, edge_send.at[i, e], edge_recv.at[i, e], tm, reg)

    def make_base(i):
        for e in range(2):
            take(edge_rows.at[i, e], edge_recv.at[i, e])
            take(edge_hours.at[i, e], edge_recv.at[i, 2 + e])
        row_low = jnp.where(r > 0, edge_rows[i, 0], 0.0)
        row_high = jnp.where(r < n_region - 1, edge_rows[i, 1], 0.0)
        hour_low = jnp.where(w > 0, edge_hours[i, 0], 0.0)
        hour_high = jnp.where(w < n_tm - 1, edge_hours[i, 1], 0.0)
        cell = lax.broadcasted_iota(jnp.int32, (ROWS, CELLS), 1)
        planes = [hour_low] + [flux[i, h] for h in range(HOURS)] + [hour_high]
        for h in range(HOURS):
            here = planes[h + 1]
            neighbours = jnp.concatenate([here[1:], row_high[h : h + 1]], axis=0)
            neighbours = neighbours + jnp.concatenate([row_low[h : h + 1], here[:-1]], axis=0)
            neighbours = neighbours + planes[h + 2] + planes[h]
            neighbours = neighbours + jnp.where(cell < CELLS - 1, pltpu.roll(here, CELLS - 1, 1), 0.0)
            neighbours = neighbours + jnp.where(cell > 0, pltpu.roll(here, 1, 1), 0.0)
            base[i, h] = here - 0.1 * (6.0 * here - neighbours)

    def stepped(start, adjoint, cutoff):
        value = start - 0.5 * adjoint
        return value - jnp.clip(value, -cutoff, cutoff)

    for i in range(ITERS):
        if i == 0:
            for l in reversed(range(LAG)):
                for reg in near_first[::-1] + ([r] if l else []):
                    send(
                        low.at[reg], window.at[0, l * n_region + r],
                        send_sem.at[0, 0], recv_sem.at[0, 0], later[l], reg,
                    )
            window[0, r] = low[r]
            for k in range(1, n_region):
                send(picks.at[r], picks.at[r], pick_sem.at[0], pick_sem.at[1], w, region[k])
            send_edges(0)
        if i == 0:
            load.wait()
            for t in range(24):
                foot_t[:, t * OBS : (t + 1) * OBS] = jnp.transpose(foot[t * OBS : (t + 1) * OBS, :])
            for h in range(HOURS):
                owned[h, 1] = (0.5 * penalty_ref[:, h, :]).astype(jnp.bfloat16)
            for l, k in others:
                send(
                    owned.at[region[k], 1], fields.at[l * n_region + r, 1],
                    side_sem.at[0, 0], side_sem.at[0, 1], later[l], region[k],
                )
            fields[r, 1] = owned[r, 1]
            take(picks.at[0 : n_region - 1], pick_sem.at[1])
            rows = picks[:, 0, :]
            columns = jnp.transpose(jnp.concatenate([rows] * 16, axis=0))
            across = lax.broadcasted_iota(jnp.int32, (SLOTS, table_rows), 1)
            for d in range(n_region):
                chosen = columns[0:SLOTS, d : d + 1] == across
                pick[d * SLOTS : (d + 1) * SLOTS, :] = chosen.astype(jnp.float32).astype(jnp.bfloat16)
            lane = lax.broadcasted_iota(jnp.int32, (1, 128), 1)
            moved = pltpu.roll(rows, SPREAD, 1)
            down = lax.broadcasted_iota(jnp.int32, (table_rows, 128), 0)
            for d in range(0, n_region, 2):
                pair = jnp.where(lane < SPREAD, rows[d : d + 1], moved[d + 1 : d + 2])
                chosen = down == pair
                pick_t[:, d * SPREAD : (d + 2) * SPREAD] = chosen.astype(jnp.float32).astype(
                    jnp.bfloat16
                )
            block_of[...] = jnp.broadcast_to(jnp.transpose(index_pad[...])[0:SLOTS, 0:1], (SLOTS, OBS))
            make_base(0)
            for h in range(HOURS):
                owned[h, 0] = base[0, h].astype(jnp.bfloat16)
            take(window.at[0, 0 : len(others)], recv_sem.at[0, 0])

        table = window[i].reshape(table_rows, CELLS)
        for q in reversed(pairs):
            rows_of = pl.ds(pl.multiple_of(q * 2 * SLOTS, 2 * SLOTS), 2 * SLOTS)
            both = dot(pick[rows_of, :], table, ((1,), (0,))).astype(jnp.bfloat16)
            blocks[i, 2 * q] = both[:SLOTS]
            blocks[i, 2 * q + 1] = both[SLOTS:]
            for reg in [2 * q + 1, 2 * q] if q is not own else [partner]:
                send(
                    blocks.at[i, reg], slots.at[i, r],
                    send_sem.at[i, 1], slot_recv.at[i, r], w, reg,
                )
        slots[i, r] = blocks[i, r]
        if i == 0:
            for l, k in others:
                send(
                    owned.at[region[k], 0], fields.at[l * n_region + r, 0],
                    side_sem.at[0, 0], side_sem.at[0, 1], later[l], region[k],
                )
            fields[r, 0] = owned[r, 0]
            for t in range(24, tiles):
                foot_t[:, t * OBS : (t + 1) * OBS] = jnp.transpose(foot[t * OBS : (t + 1) * OBS, :])
        else:
            for reg in reversed(near_first):
                send(whole_out.at[reg], whole_in.at[r], side_sem.at[1, 0], side_sem.at[1, 1], w, reg)
            whole_in[r] = whole_out[r]

        down = lax.broadcasted_iota(jnp.int32, (GROUP, OBS), 0)
        groups = [(first, min(first + GROUP, tiles)) for first in range(0, SLOTS, GROUP)]
        products = [jnp.zeros((GROUP, OBS), jnp.float32) for _ in groups]
        for step, q in enumerate(pairs):
            for reg in [2 * q, 2 * q + 1] if step else [partner]:
                take(slots.at[i, reg], slot_recv.at[i, reg])
            x = jnp.concatenate([slots[i, 2 * q], slots[i, 2 * q + 1]], axis=1)
            cells = pl.ds(pl.multiple_of(q * 2 * CELLS, 2 * CELLS), 2 * CELLS)
            for g, (first, last) in enumerate(groups):
                x_group = x[first : first + GROUP, :]
                total = jnp.zeros((GROUP, OBS), jnp.float32)
                for t in range(first, last, 2):
                    both = dot(x_group, foot_t[cells, t * OBS : (t + 2) * OBS], ((1,), (0,)))
                    total = jnp.where(down == t - first, both[:, :OBS], total)
                    total = jnp.where(down == t + 1 - first, both[:, OBS:], total)
                products[g] = products[g] + total
        products = jnp.concatenate(products, axis=0)
        residual = []
        for b in range(NOB):
            predicted = jnp.sum(jnp.where(block_of[...] == b, products, 0.0), axis=0, keepdims=True)
            residual.append(
                (predicted - observed_ref[b : b + 1, :]).astype(jnp.bfloat16).astype(jnp.float32)
            )

        spread = jnp.zeros((SLOTS, OBS), jnp.float32)
        for b in range(NOB):
            spread = jnp.where(block_of[...] == b, residual[b], spread)
        lefts = []
        for first in range(0, SLOTS, GROUP):
            part = spread[first : first + GROUP, :]
            lefts.append(
                jnp.concatenate(
                    [
                        jnp.where(down == t - first, part, 0.0)
                        for t in range(first, min(first + GROUP, tiles))
                    ],
                    axis=1,
                ).astype(jnp.bfloat16)
            )
        for q in reversed(pairs):
            cells = pl.ds(pl.multiple_of(q * 2 * CELLS, 2 * CELLS), 2 * CELLS)
            for g, (first, last) in enumerate(groups):
                both = dot(
                    lefts[g], foot[first * OBS : last * OBS, cells], ((1,), (0,))
                ).astype(jnp.bfloat16)
                terms[i, 2 * q, first : first + GROUP, :] = both[:, :CELLS]
                terms[i, 2 * q + 1, first : first + GROUP, :] = both[:, CELLS:]
            for reg in [2 * q, 2 * q + 1] if q is not own else [partner]:
                send(
                    terms.at[i, reg], all_terms.at[i, r, 0:SLOTS],
                    send_sem.at[i, 2], recv_sem.at[i, 2], w, reg,
                )
        all_terms[i, r, 0:SLOTS] = terms[i, r]
        if i > 0:
            take(whole_in.at[0 : n_region - 1], side_sem.at[1, 1])
            for h in range(HOURS):
                flux[i, h] = stepped(base[i - 1, h], whole_in[h], 0.5 * penalty_ref[:, h, :])
            send_edges(i)
        take(all_terms.at[i, 0 : n_region - 1, 0:SLOTS], recv_sem.at[i, 2])

        received = all_terms[i].reshape(n_region * SPREAD, CELLS)
        lag_rows = n_region * ROWS
        at, later_at, earlier_at = 0, {}, {}
        for d in range(1, LAG):
            size = (LAG - d) * n_region
            later_at[d], earlier_at[d] = at, at + size
            at += 2 * size
        ready = set()
        waiting = [(d, side) for d in reversed(range(1, LAG)) for side in (0, 1)]
        for l in [3, 0, 1, 2] if i < ITERS - 1 else [3, 2, 1, 0]:
            part = dot(pick_t[l * lag_rows : (l + 1) * lag_rows, :], received, ((1,), (0,)))
            sums[i, l * n_region : (l + 1) * n_region] = part.astype(jnp.bfloat16).reshape(
                n_region, ROWS, CELLS
            )
            ready.add(l)
            for d, side in list(waiting) if i < ITERS - 1 else []:
                first = d * side
                if not ready.issuperset(range(first, first + LAG - d)):
                    continue
                waiting.remove((d, side))
                size = (LAG - d) * n_region
                start = earlier_at[d] if side else later_at[d]
                send(
                    sums.at[i, first * n_region : first * n_region + size],
                    nearby.at[start : start + size],
                    side_sem.at[2, 0], side_sem.at[2, 1], earlier[d] if side else later[d], r,
                )
            if i == ITERS - 1:
                for reg in near_first[::-1] + ([r] if l else []):
                    send(
                        sums.at[i, l * n_region + reg], parts.at[l * n_region + r],
                        send_sem.at[i, 3], recv_sem.at[i, 3], earlier[l], reg,
                    )
        if i < ITERS - 1:
            take(fields.at[0 : len(others)], side_sem.at[0, 1])
            take(nearby, side_sem.at[2, 1])
            for l in range(LAG):
                rows_of = [(nearby, later_at[d] + (l - d) * n_region) for d in range(1, l + 1)]
                rows_of += [(nearby, earlier_at[d] + l * n_region) for d in range(1, LAG - l)]
                for g in range(n_region):
                    adjoint = sums[i, l * n_region + g].astype(jnp.float32)
                    for ref, start in rows_of:
                        adjoint = adjoint + ref[start + g].astype(jnp.float32)
                    if l == 0:
                        whole_out[g] = adjoint
                    field = fields[l * n_region + g].astype(jnp.float32)
                    window[i + 1, l * n_region + g] = stepped(field[0], adjoint, field[1]).astype(
                        jnp.bfloat16
                    )
        else:
            parts[r] = sums[i, r]
            make_base(i)
            take(parts.at[0 : len(others)], recv_sem.at[i, 3])
            for h in range(HOURS):
                adjoint = parts[h].astype(jnp.float32)
                for l in range(1, LAG):
                    adjoint = adjoint + parts[l * n_region + h].astype(jnp.float32)
                out_ref[:, h, :] = base[i, h] - 0.5 * adjoint

    take(picks.at[0 : n_region - 1], pick_sem.at[0])
    take(window.at[0, 0 : len(others)], send_sem.at[0, 0])
    take(fields.at[0 : len(others)], side_sem.at[0, 0])
    take(whole_in.at[0 : n_region - 1], side_sem.at[1, 0])
    take(nearby, side_sem.at[2, 0])
    take(parts.at[0 : len(others)], send_sem.at[ITERS - 1, 3])
    for i in range(ITERS):
        take(slots.at[i, 0 : n_region - 1], send_sem.at[i, 1])
        take(terms.at[i, 0 : n_region - 1], send_sem.at[i, 2])
        for e in range(2):
            take(edge_rows.at[i, e], edge_send.at[i, e])
            take(edge_hours.at[i, e], edge_send.at[i, 2 + e])


def local(flux_init, penalty, observed, footprint, tile_index):
    n_tm, n_region = lax.axis_size("tm"), lax.axis_size("region")
    tiles = tile_index.shape[0]
    in_vmem = pl.BlockSpec(memory_space=pltpu.VMEM)
    table = LAG * n_region
    half, full = jnp.bfloat16, jnp.float32
    dma = pltpu.SemaphoreType.DMA
    last = pl.pallas_call(
        functools.partial(kernel, n_tm, n_region, tiles),
        out_shape=jax.ShapeDtypeStruct(flux_init.shape, full),
        in_specs=[pl.BlockSpec(memory_space=pltpu.HBM)] * 5,
        out_specs=in_vmem,
        scratch_shapes=[
            pltpu.VMEM(flux_init.shape, full),
            pltpu.VMEM(flux_init.shape, full),
            pltpu.VMEM((NOB, OBS), full),
            pltpu.VMEM((4, tiles), jnp.int32),
            pltpu.VMEM((tiles * OBS, HOURS * CELLS), half),
            pltpu.VMEM((HOURS * CELLS, tiles * OBS), half),
            pltpu.VMEM((ITERS, HOURS, ROWS, CELLS), full),
            pltpu.VMEM((HOURS, ROWS, CELLS), half),
            pltpu.VMEM((ITERS, table, ROWS, CELLS), half),
            pltpu.VMEM((ITERS, n_region, SLOTS, CELLS), half),
            pltpu.VMEM((ITERS, n_region, SLOTS, CELLS), half),
            pltpu.VMEM((ITERS, n_region, SLOTS, CELLS), half),
            pltpu.VMEM((ITERS, n_region, SPREAD, CELLS), half),
            pltpu.VMEM((ITERS, table, ROWS, CELLS), half),
            pltpu.VMEM((table, ROWS, CELLS), half),
            pltpu.VMEM((ITERS, HOURS, ROWS, CELLS), full),
            pltpu.VMEM((HOURS, 2, ROWS, CELLS), half),
            pltpu.VMEM((table, 2, ROWS, CELLS), half),
            pltpu.VMEM((LAG * (LAG - 1) * n_region, ROWS, CELLS), half),
            pltpu.VMEM((n_region, ROWS, CELLS), full),
            pltpu.VMEM((n_region, ROWS, CELLS), full),
            pltpu.VMEM((ITERS, 2, HOURS, CELLS), full),
            pltpu.VMEM((ITERS, 2, HOURS, CELLS), full),
            pltpu.VMEM((ITERS, 2, ROWS, CELLS), full),
            pltpu.VMEM((128, 128), jnp.int32),
            pltpu.VMEM((SLOTS, OBS), jnp.int32),
            pltpu.VMEM((n_region, 8, 128), jnp.int32),
            pltpu.VMEM((n_region * SLOTS, table * ROWS), half),
            pltpu.VMEM((table * ROWS, n_region * SPREAD), half),
            dma,
            dma((4,)),
            dma((2,)),
            dma((ITERS, 4)),
            dma((ITERS, 4)),
            dma((ITERS, n_region)),
            dma((3, 2)),
            dma((ITERS, 4)),
            dma((ITERS, 4)),
        ],
        compiler_params=pltpu.CompilerParams(
            collective_id=0, has_side_effects=True, vmem_limit_bytes=55 * 2**20
        ),
        cost_estimate=pl.CostEstimate(
            flops=8 * footprint.size, bytes_accessed=2 * footprint.size, transcendentals=0
        ),
    )(
        flux_init,
        penalty,
        observed.reshape(NOB, OBS),
        tile_index.T,
        footprint.reshape(tiles * OBS, HOURS * CELLS),
    )
    cutoff = 0.5 * penalty
    return last - jnp.clip(last, -cutoff, cutoff)


def solution(mesh):
    in_specs = (
        P("region", "tm", None),
        P("region", "tm", None),
        P(("tm", "region")),
        P(("tm", "region"), None, None),
        P(("tm", "region"), None),
    )
    out_specs = P("region", "tm", None)
    return jax.shard_map(local, mesh=mesh, in_specs=in_specs, out_specs=out_specs, check_vma=False)
```

```python
import functools

import jax
import jax.numpy as jnp
from jax import lax
from jax.experimental import pallas as pl
from jax.experimental.pallas import tpu as pltpu
from jax.sharding import PartitionSpec as P

LAG = 4
ITERS = 2
SLOTS = 48
SPREAD = 64
ROWS = 16
HOURS = 8
CELLS = 128
OBS = 128
NOB = 8
GROUP = 16
MESH = pl.DeviceIdType.MESH


def take(ref, sem):
    pltpu.make_async_copy(ref, ref, sem).wait()


def dot(a, b, dims):
    return lax.dot_general(a, b, (dims, ((), ())), preferred_element_type=jnp.float32)


def kernel(
    n_tm,
    n_region,
    tiles,
    flux_hbm,
    penalty_hbm,
    observed_hbm,
    index_hbm,
    footprint_ref,
    out_ref,
    flux_ref,
    penalty_ref,
    observed_ref,
    index_ref,
    foot,
    foot_t,
    flux,
    low,
    window,
    blocks,
    slots,
    terms,
    all_terms,
    sums,
    parts,
    base,
    owned,
    fields,
    nearby,
    whole_out,
    whole_in,
    edges,
    edge_rows,
    edge_hours,
    index_pad,
    block_of,
    picks,
    pick,
    pick_t,
    foot_sem,
    input_sem,
    pick_sem,
    send_sem,
    recv_sem,
    slot_recv,
    side_sem,
    edge_send,
    edge_recv,
):
    w = lax.axis_index("tm")
    r = lax.axis_index("region")
    later = [lax.rem(w + l, n_tm) for l in range(LAG)]
    earlier = [lax.rem(w + n_tm - l, n_tm) for l in range(LAG)]
    region = [lax.rem(r + k, n_region) for k in range(n_region)]
    others = [(l, k) for l in reversed(range(LAG)) for k in range(n_region) if (l, k) != (0, 0)]
    table_rows = LAG * n_region * ROWS
    own = r // 2
    flip = own + 1 - 2 * lax.rem(own, 2)
    pairs = [own, flip, lax.rem(own + 2, 4), lax.rem(flip + 2, 4)]
    partner = r + 1 - 2 * lax.rem(r, 2)
    near_first = [partner] + [2 * q + e for q in pairs[1:] for e in range(2)]

    barrier = pltpu.get_barrier_semaphore()
    for l, k in others:
        pl.semaphore_signal(
            barrier, inc=1, device_id={"tm": earlier[l], "region": region[k]}, device_id_type=MESH
        )
    pl.semaphore_signal(barrier, inc=1, device_id={"tm": later[1], "region": r}, device_id_type=MESH)

    inputs = [
        pltpu.make_async_copy(src, dst, input_sem.at[k])
        for k, (src, dst) in enumerate(
            [
                (flux_hbm, flux_ref),
                (index_hbm, index_ref),
                (observed_hbm, observed_ref),
                (penalty_hbm, penalty_ref),
            ]
        )
    ]
    load = pltpu.make_async_copy(footprint_ref, foot, foot_sem)
    for copy in inputs + [load]:
        copy.start()

    def send(src, dst, sent, received, tm, reg):
        pltpu.make_async_remote_copy(
            src_ref=src,
            dst_ref=dst,
            send_sem=sent,
            recv_sem=received,
            device_id={"tm": tm, "region": reg},
            device_id_type=MESH,
        ).start()

    inputs[0].wait()
    for h in range(HOURS):
        flux[0, h] = flux_ref[:, h, :]
        low[h] = flux[0, h].astype(jnp.bfloat16)

    pl.semaphore_wait(barrier, len(others) + 1)

    def send_edges(i):
        edges[i, 0] = flux[i, :, 0, :]
        edges[i, 1] = flux[i, :, ROWS - 1, :]
        for e, (src, dst, tm, reg) in enumerate(
            [
                (edges.at[i, 1], edge_rows.at[i, 0], w, region[1]),
                (edges.at[i, 0], edge_rows.at[i, 1], w, region[n_region - 1]),
                (flux.at[i, HOURS - 1], edge_hours.at[i, 0], later[1], r),
                (flux.at[i, 0], edge_hours.at[i, 1], earlier[1], r),
            ]
        ):
            send(src, dst, edge_send.at[i, e], edge_recv.at[i, e], tm, reg)

    def make_base(i):
        for e in range(2):
            take(edge_rows.at[i, e], edge_recv.at[i, e])
            take(edge_hours.at[i, e], edge_recv.at[i, 2 + e])
        row_low = jnp.where(r > 0, edge_rows[i, 0], 0.0)
        row_high = jnp.where(r < n_region - 1, edge_rows[i, 1], 0.0)
        hour_low = jnp.where(w > 0, edge_hours[i, 0], 0.0)
        hour_high = jnp.where(w < n_tm - 1, edge_hours[i, 1], 0.0)
        cell = lax.broadcasted_iota(jnp.int32, (ROWS, CELLS), 1)
        planes = [hour_low] + [flux[i, h] for h in range(HOURS)] + [hour_high]
        for h in range(HOURS):
            here = planes[h + 1]
            neighbours = jnp.concatenate([here[1:], row_high[h : h + 1]], axis=0)
            neighbours = neighbours + jnp.concatenate([row_low[h : h + 1], here[:-1]], axis=0)
            neighbours = neighbours + planes[h + 2] + planes[h]
            neighbours = neighbours + jnp.where(cell < CELLS - 1, pltpu.roll(here, CELLS - 1, 1), 0.0)
            neighbours = neighbours + jnp.where(cell > 0, pltpu.roll(here, 1, 1), 0.0)
            base[i, h] = here - 0.1 * (6.0 * here - neighbours)

    def stepped(start, adjoint, cutoff):
        value = start - 0.5 * adjoint
        return value - jnp.clip(value, -cutoff, cutoff)

    for i in range(ITERS):
        if i == 0:
            for l in reversed(range(LAG)):
                for reg in near_first[::-1] + ([r] if l else []):
                    send(
                        low.at[reg], window.at[0, l * n_region + r],
                        send_sem.at[0, 0], recv_sem.at[0, 0], later[l], reg,
                    )
            window[0, r] = low[r]
            index_pad[...] = jnp.zeros_like(index_pad)
            inputs[1].wait()
            index_pad[0:4, 0:tiles] = index_ref[...]
            entries = index_pad[...]
            lag = entries[1:2, :]
            usable = (entries[3:4, :] == 1) & (lag <= w)
            mine = jnp.where(usable, lag * (n_region * ROWS) + entries[2:3, :], -1)
            picks[r] = jnp.broadcast_to(mine, (8, 128))
            for k in range(1, n_region):
                send(picks.at[r], picks.at[r], pick_sem.at[0], pick_sem.at[1], w, region[k])
            send_edges(0)
            all_terms[...] = jnp.zeros_like(all_terms)
            for copy in inputs[2:]:
                copy.wait()
        if i == 0:
            load.wait()
            for t in range(24):
                foot_t[:, t * OBS : (t + 1) * OBS] = jnp.transpose(foot[t * OBS : (t + 1) * OBS, :])
            for h in range(HOURS):
                owned[h, 1] = (0.5 * penalty_ref[:, h, :]).astype(jnp.bfloat16)
            for l, k in others:
                send(
                    owned.at[region[k], 1], fields.at[l * n_region + r, 1],
                    side_sem.at[0, 0], side_sem.at[0, 1], later[l], region[k],
                )
            fields[r, 1] = owned[r, 1]
            take(picks.at[0 : n_region - 1], pick_sem.at[1])
            rows = picks[:, 0, :]
            columns = jnp.transpose(jnp.concatenate([rows] * 16, axis=0))
            across = lax.broadcasted_iota(jnp.int32, (SLOTS, table_rows), 1)
            for d in range(n_region):
                chosen = columns[0:SLOTS, d : d + 1] == across
                pick[d * SLOTS : (d + 1) * SLOTS, :] = chosen.astype(jnp.float32).astype(jnp.bfloat16)
            lane = lax.broadcasted_iota(jnp.int32, (1, 128), 1)
            moved = pltpu.roll(rows, SPREAD, 1)
            down = lax.broadcasted_iota(jnp.int32, (table_rows, 128), 0)
            for d in range(0, n_region, 2):
                pair = jnp.where(lane < SPREAD, rows[d : d + 1], moved[d + 1 : d + 2])
                chosen = down == pair
                pick_t[:, d * SPREAD : (d + 2) * SPREAD] = chosen.astype(jnp.float32).astype(
                    jnp.bfloat16
                )
            block_of[...] = jnp.broadcast_to(jnp.transpose(index_pad[...])[0:SLOTS, 0:1], (SLOTS, OBS))
            make_base(0)
            for h in range(HOURS):
                owned[h, 0] = base[0, h].astype(jnp.bfloat16)
            take(window.at[0, 0 : len(others)], recv_sem.at[0, 0])

        table = window[i].reshape(table_rows, CELLS)
        for q in reversed(pairs):
            rows_of = pl.ds(pl.multiple_of(q * 2 * SLOTS, 2 * SLOTS), 2 * SLOTS)
            both = dot(pick[rows_of, :], table, ((1,), (0,))).astype(jnp.bfloat16)
            blocks[i, 2 * q] = both[:SLOTS]
            blocks[i, 2 * q + 1] = both[SLOTS:]
            for reg in [2 * q + 1, 2 * q] if q is not own else [partner]:
                send(
                    blocks.at[i, reg], slots.at[i, r],
                    send_sem.at[i, 1], slot_recv.at[i, r], w, reg,
                )
        slots[i, r] = blocks[i, r]
        if i == 0:
            for l, k in others:
                send(
                    owned.at[region[k], 0], fields.at[l * n_region + r, 0],
                    side_sem.at[0, 0], side_sem.at[0, 1], later[l], region[k],
                )
            fields[r, 0] = owned[r, 0]
            for t in range(24, tiles):
                foot_t[:, t * OBS : (t + 1) * OBS] = jnp.transpose(foot[t * OBS : (t + 1) * OBS, :])
        else:
            for reg in reversed(near_first):
                send(whole_out.at[reg], whole_in.at[r], side_sem.at[1, 0], side_sem.at[1, 1], w, reg)
            whole_in[r] = whole_out[r]

        down = lax.broadcasted_iota(jnp.int32, (GROUP, OBS), 0)
        groups = [(first, min(first + GROUP, tiles)) for first in range(0, SLOTS, GROUP)]
        products = [jnp.zeros((GROUP, OBS), jnp.float32) for _ in groups]
        for step, q in enumerate(pairs):
            for reg in [2 * q, 2 * q + 1] if step else [partner]:
                take(slots.at[i, reg], slot_recv.at[i, reg])
            x = jnp.concatenate([slots[i, 2 * q], slots[i, 2 * q + 1]], axis=1)
            cells = pl.ds(pl.multiple_of(q * 2 * CELLS, 2 * CELLS), 2 * CELLS)
            for g, (first, last) in enumerate(groups):
                x_group = x[first : first + GROUP, :]
                total = jnp.zeros((GROUP, OBS), jnp.float32)
                for t in range(first, last, 2):
                    both = dot(x_group, foot_t[cells, t * OBS : (t + 2) * OBS], ((1,), (0,)))
                    total = jnp.where(down == t - first, both[:, :OBS], total)
                    total = jnp.where(down == t + 1 - first, both[:, OBS:], total)
                products[g] = products[g] + total
        products = jnp.concatenate(products, axis=0)
        residual = []
        for b in range(NOB):
            predicted = jnp.sum(jnp.where(block_of[...] == b, products, 0.0), axis=0, keepdims=True)
            residual.append(
                (predicted - observed_ref[b : b + 1, :]).astype(jnp.bfloat16).astype(jnp.float32)
            )

        spread = jnp.zeros((SLOTS, OBS), jnp.float32)
        for b in range(NOB):
            spread = jnp.where(block_of[...] == b, residual[b], spread)
        lefts = []
        for first in range(0, SLOTS, GROUP):
            part = spread[first : first + GROUP, :]
            lefts.append(
                jnp.concatenate(
                    [
                        jnp.where(down == t - first, part, 0.0)
                        for t in range(first, min(first + GROUP, tiles))
                    ],
                    axis=1,
                ).astype(jnp.bfloat16)
            )
        for q in reversed(pairs):
            cells = pl.ds(pl.multiple_of(q * 2 * CELLS, 2 * CELLS), 2 * CELLS)
            for g, (first, last) in enumerate(groups):
                both = dot(
                    lefts[g], foot[first * OBS : last * OBS, cells], ((1,), (0,))
                ).astype(jnp.bfloat16)
                terms[i, 2 * q, first : first + GROUP, :] = both[:, :CELLS]
                terms[i, 2 * q + 1, first : first + GROUP, :] = both[:, CELLS:]
            for reg in [2 * q, 2 * q + 1] if q is not own else [partner]:
                send(
                    terms.at[i, reg], all_terms.at[i, r, 0:SLOTS],
                    send_sem.at[i, 2], recv_sem.at[i, 2], w, reg,
                )
        all_terms[i, r, 0:SLOTS] = terms[i, r]
        if i > 0:
            take(whole_in.at[0 : n_region - 1], side_sem.at[1, 1])
            for h in range(HOURS):
                flux[i, h] = stepped(base[i - 1, h], whole_in[h], 0.5 * penalty_ref[:, h, :])
            send_edges(i)
        take(all_terms.at[i, 0 : n_region - 1, 0:SLOTS], recv_sem.at[i, 2])

        received = all_terms[i].reshape(n_region * SPREAD, CELLS)
        lag_rows = n_region * ROWS
        at, later_at, earlier_at = 0, {}, {}
        for d in range(1, LAG):
            size = (LAG - d) * n_region
            later_at[d], earlier_at[d] = at, at + size
            at += 2 * size
        ready = set()
        waiting = [(d, side) for d in reversed(range(1, LAG)) for side in (0, 1)]
        for l in [3, 0, 1, 2] if i < ITERS - 1 else [3, 2, 1, 0]:
            part = dot(pick_t[l * lag_rows : (l + 1) * lag_rows, :], received, ((1,), (0,)))
            sums[i, l * n_region : (l + 1) * n_region] = part.astype(jnp.bfloat16).reshape(
                n_region, ROWS, CELLS
            )
            ready.add(l)
            for d, side in list(waiting) if i < ITERS - 1 else []:
                first = d * side
                if not ready.issuperset(range(first, first + LAG - d)):
                    continue
                waiting.remove((d, side))
                size = (LAG - d) * n_region
                start = earlier_at[d] if side else later_at[d]
                send(
                    sums.at[i, first * n_region : first * n_region + size],
                    nearby.at[start : start + size],
                    side_sem.at[2, 0], side_sem.at[2, 1], earlier[d] if side else later[d], r,
                )
            if i == ITERS - 1:
                for reg in near_first[::-1] + ([r] if l else []):
                    send(
                        sums.at[i, l * n_region + reg], parts.at[l * n_region + r],
                        send_sem.at[i, 3], recv_sem.at[i, 3], earlier[l], reg,
                    )
        if i < ITERS - 1:
            take(fields.at[0 : len(others)], side_sem.at[0, 1])
            take(nearby, side_sem.at[2, 1])
            for l in range(LAG):
                rows_of = [(nearby, later_at[d] + (l - d) * n_region) for d in range(1, l + 1)]
                rows_of += [(nearby, earlier_at[d] + l * n_region) for d in range(1, LAG - l)]
                for g in range(n_region):
                    adjoint = sums[i, l * n_region + g].astype(jnp.float32)
                    for ref, start in rows_of:
                        adjoint = adjoint + ref[start + g].astype(jnp.float32)
                    if l == 0:
                        whole_out[g] = adjoint
                    field = fields[l * n_region + g].astype(jnp.float32)
                    window[i + 1, l * n_region + g] = stepped(field[0], adjoint, field[1]).astype(
                        jnp.bfloat16
                    )
        else:
            parts[r] = sums[i, r]
            make_base(i)
            take(parts.at[0 : len(others)], recv_sem.at[i, 3])
            for h in range(HOURS):
                adjoint = parts[h].astype(jnp.float32)
                for l in range(1, LAG):
                    adjoint = adjoint + parts[l * n_region + h].astype(jnp.float32)
                out_ref[:, h, :] = base[i, h] - 0.5 * adjoint

    take(picks.at[0 : n_region - 1], pick_sem.at[0])
    take(window.at[0, 0 : len(others)], send_sem.at[0, 0])
    take(fields.at[0 : len(others)], side_sem.at[0, 0])
    take(whole_in.at[0 : n_region - 1], side_sem.at[1, 0])
    take(nearby, side_sem.at[2, 0])
    take(parts.at[0 : len(others)], send_sem.at[ITERS - 1, 3])
    for i in range(ITERS):
        take(slots.at[i, 0 : n_region - 1], send_sem.at[i, 1])
        take(terms.at[i, 0 : n_region - 1], send_sem.at[i, 2])
        for e in range(2):
            take(edge_rows.at[i, e], edge_send.at[i, e])
            take(edge_hours.at[i, e], edge_send.at[i, 2 + e])


def local(flux_init, penalty, observed, footprint, tile_index):
    n_tm, n_region = lax.axis_size("tm"), lax.axis_size("region")
    tiles = tile_index.shape[0]
    in_vmem = pl.BlockSpec(memory_space=pltpu.VMEM)
    table = LAG * n_region
    half, full = jnp.bfloat16, jnp.float32
    dma = pltpu.SemaphoreType.DMA
    last = pl.pallas_call(
        functools.partial(kernel, n_tm, n_region, tiles),
        out_shape=jax.ShapeDtypeStruct(flux_init.shape, full),
        in_specs=[pl.BlockSpec(memory_space=pltpu.HBM)] * 5,
        out_specs=in_vmem,
        scratch_shapes=[
            pltpu.VMEM(flux_init.shape, full),
            pltpu.VMEM(flux_init.shape, full),
            pltpu.VMEM((NOB, OBS), full),
            pltpu.VMEM((4, tiles), jnp.int32),
            pltpu.VMEM((tiles * OBS, HOURS * CELLS), half),
            pltpu.VMEM((HOURS * CELLS, tiles * OBS), half),
            pltpu.VMEM((ITERS, HOURS, ROWS, CELLS), full),
            pltpu.VMEM((HOURS, ROWS, CELLS), half),
            pltpu.VMEM((ITERS, table, ROWS, CELLS), half),
            pltpu.VMEM((ITERS, n_region, SLOTS, CELLS), half),
            pltpu.VMEM((ITERS, n_region, SLOTS, CELLS), half),
            pltpu.VMEM((ITERS, n_region, SLOTS, CELLS), half),
            pltpu.VMEM((ITERS, n_region, SPREAD, CELLS), half),
            pltpu.VMEM((ITERS, table, ROWS, CELLS), half),
            pltpu.VMEM((table, ROWS, CELLS), half),
            pltpu.VMEM((ITERS, HOURS, ROWS, CELLS), full),
            pltpu.VMEM((HOURS, 2, ROWS, CELLS), half),
            pltpu.VMEM((table, 2, ROWS, CELLS), half),
            pltpu.VMEM((LAG * (LAG - 1) * n_region, ROWS, CELLS), half),
            pltpu.VMEM((n_region, ROWS, CELLS), full),
            pltpu.VMEM((n_region, ROWS, CELLS), full),
            pltpu.VMEM((ITERS, 2, HOURS, CELLS), full),
            pltpu.VMEM((ITERS, 2, HOURS, CELLS), full),
            pltpu.VMEM((ITERS, 2, ROWS, CELLS), full),
            pltpu.VMEM((128, 128), jnp.int32),
            pltpu.VMEM((SLOTS, OBS), jnp.int32),
            pltpu.VMEM((n_region, 8, 128), jnp.int32),
            pltpu.VMEM((n_region * SLOTS, table * ROWS), half),
            pltpu.VMEM((table * ROWS, n_region * SPREAD), half),
            dma,
            dma((4,)),
            dma((2,)),
            dma((ITERS, 4)),
            dma((ITERS, 4)),
            dma((ITERS, n_region)),
            dma((3, 2)),
            dma((ITERS, 4)),
            dma((ITERS, 4)),
        ],
        compiler_params=pltpu.CompilerParams(
            collective_id=0, has_side_effects=True, vmem_limit_bytes=55 * 2**20
        ),
        cost_estimate=pl.CostEstimate(
            flops=8 * footprint.size, bytes_accessed=2 * footprint.size, transcendentals=0
        ),
    )(
        flux_init,
        penalty,
        observed.reshape(NOB, OBS),
        tile_index.T,
        footprint.reshape(tiles * OBS, HOURS * CELLS),
    )
    cutoff = 0.5 * penalty
    return last - jnp.clip(last, -cutoff, cutoff)


def solution(mesh):
    in_specs = (
        P("region", "tm", None),
        P("region", "tm", None),
        P(("tm", "region")),
        P(("tm", "region"), None, None),
        P(("tm", "region"), None),
    )
    out_specs = P("region", "tm", None)
    return jax.shard_map(local, mesh=mesh, in_specs=in_specs, out_specs=out_specs, check_vma=False)
```
